32 devices in a mesh: chan: 8 (over y, x, core), seg: 4 (over z).
Axes of the slice: x: 2, y: 2, z: 4, core: 2. Of those that a mesh axis runs over, the one named last changes fastest.
Arguments:
- spectra: bfloat16 [2, 32, 256, 512], P(None, 'seg', 'chan'), may hold values from -6 to 6
- sources: int32 [8, 4], replicated, may hold values from 0 to 255, as said below
Outputs:
- correlations: float32 [32, 256, 512], P(None, ('chan', 'seg'))
The draws below stay inside these ranges and needn't reach their ends.
Inputs may be any that keep to these rules, and one draw needn't show every extreme that they name: `sources`: each entry names a channel of the array; entries may repeat and may crowd onto the channels of a few devices of chan.
All inputs are finite; a program needn't handle non-finite values.
Results may differ from the reference program's by a relative error of at most 0.004.
Values may be sent and summed in bfloat16 or wider, within the bound.
A program may use at most 128 MiB of HBM per device.

```python
import math
import jax
import jax.numpy as jnp
from jax import lax

FREQS = 512
LAGS = 256
CH_DEV = 32
BATCHES = 8
PER_BATCH = 4
CHANNELS = 256
SEGMENTS = 32
SOURCES = 32


def draw_sources(key, part):
    owners_count = CHANNELS // CH_DEV
    keys = jax.random.split(jax.random.fold_in(key, 7), 5)
    hubs = jax.random.randint(keys[0], (4,), 0, owners_count)
    pick = jax.random.randint(keys[1], (BATCHES, PER_BATCH), 0, 4)
    crowded = hubs[pick]
    anywhere = jax.random.randint(keys[2], (BATCHES, PER_BATCH), 0, owners_count)
    use_hub = jax.random.randint(keys[3], (BATCHES, PER_BATCH), 0, 2) == 1
    owner = jnp.where(use_hub, crowded, anywhere)
    offset = jax.random.randint(keys[4], (BATCHES, PER_BATCH), 0, CH_DEV)
    return (owner * CH_DEV + offset).astype(jnp.int32)


def level_of(key, shape, cuts, smallest, largest):
    def one(position, parts):
        heights = jax.random.uniform(jax.random.fold_in(jax.random.fold_in(key, 6), position), (parts,), jnp.float32, smallest / len(cuts), largest / len(cuts))
        return jnp.repeat(jnp.exp(heights), shape[position] // parts).reshape((-1,) + (1,) * (len(shape) - position - 1))

    loudness = one(*cuts[0])
    for cut in cuts[1:]:
        loudness = loudness * one(*cut)
    return loudness


def scatter_about(own_key, dims, deviation, most, cuts=(), held_as=jnp.bfloat16):
    values = jax.random.normal(own_key, dims, jnp.float32) * deviation
    if len(cuts) > 0:
        values = level_of(own_key, dims, cuts, -0.22, 0.18) * values
    return jnp.clip(values, min=-most, max=most).astype(held_as)


def setup_inputs(seed: int = 0) -> dict:
    splits = jax.random.split(jax.random.key(seed), 3)
    return {
        "spectra": scatter_about(splits[0], (2, SEGMENTS, CHANNELS, FREQS), 1.0, 6.0, ((1, 4), (2, 8))),
        "sources": draw_sources(jax.random.fold_in(splits[2], 71), 0),
    }


def whiten(spectra):
    values = spectra.astype(jnp.float32)
    power_mean = lax.optimization_barrier(jnp.mean(values[0] * values[0] + values[1] * values[1], axis=-1))
    inv_scale = lax.rsqrt(power_mean + 1e-06)
    return (values * inv_scale[None, :, :, None]).astype(jnp.bfloat16)

def lag_matrix(freqs, half_lags):
    period = 2 * freqs
    rows = jnp.arange(freqs, dtype=jnp.int32)
    shifts = jnp.arange(2 * half_lags, dtype=jnp.int32) - half_lags
    phase = jnp.mod(rows[:, None] * shifts[None, :], period)
    angles = phase.astype(jnp.float32) * (2.0 * math.pi / period)
    return jnp.concatenate([jnp.cos(angles), -jnp.sin(angles)], axis=0)

def correlate_ref(source_spec, receiver_spec, lag_table):
    segs = receiver_spec.shape[1]
    freqs = receiver_spec.shape[3]
    high = lax.Precision.HIGHEST
    real_part = jnp.einsum('pkf,krf->prf', source_spec[0], receiver_spec[0], precision=high) + jnp.einsum('pkf,krf->prf', source_spec[1], receiver_spec[1], precision=high)
    imag_part = jnp.einsum('pkf,krf->prf', source_spec[0], receiver_spec[1], precision=high) - jnp.einsum('pkf,krf->prf', source_spec[1], receiver_spec[0], precision=high)
    stacked = jnp.concatenate([real_part, imag_part], axis=-1) * (1.0 / math.sqrt(segs))
    flat = stacked.reshape(-1, 2 * freqs)
    result = jnp.dot(flat, lag_table, precision=high, preferred_element_type=jnp.float32) * (1.0 / math.sqrt(freqs))
    return result.reshape(stacked.shape[0], stacked.shape[1], -1)

def reference(spectra, sources):
    blocks_count = CHANNELS // CH_DEV
    blocks = spectra.reshape(2, SEGMENTS, blocks_count, CH_DEV, FREQS).transpose(2, 0, 1, 3, 4)
    whitened = lax.map(whiten, blocks).transpose(1, 2, 0, 3, 4).reshape(2, SEGMENTS, CHANNELS, FREQS)
    lag_table = lag_matrix(FREQS, LAGS)

    def one_batch(ids):
        chosen = jnp.take(whitened, ids, axis=2)
        chosen = jnp.transpose(chosen, (0, 2, 1, 3)).astype(jnp.float32)

        def one_block(start):
            receivers = lax.dynamic_slice_in_dim(whitened, start, CH_DEV, 2).astype(jnp.float32)
            return correlate_ref(chosen, receivers, lag_table)
        starts = jnp.arange(blocks_count, dtype=jnp.int32) * CH_DEV
        pieces = lax.map(one_block, starts)
        return jnp.transpose(pieces, (1, 0, 2, 3)).reshape(PER_BATCH, CHANNELS, 2 * LAGS)
    output = lax.map(one_batch, sources)
    return output.reshape(SOURCES, CHANNELS, 2 * LAGS)
```

```python
import functools
import math

import jax
import jax.numpy as jnp
import ml_dtypes
import numpy as np
from jax import lax
from jax.experimental import pallas as pl
from jax.experimental.pallas import tpu as pltpu
from jax.sharding import PartitionSpec as P

LAGS = 256
MESH = pl.DeviceIdType.MESH


def whiten(spectra):
    values = spectra.astype(jnp.float32)
    power_mean = jnp.mean(values[0] * values[0] + values[1] * values[1], axis=-1)
    inv_scale = lax.rsqrt(power_mean + 1e-06)
    return (values * inv_scale[None, :, :, None]).astype(jnp.bfloat16)


def lag_matrix(freqs, half_lags):
    period = 2 * freqs
    rows = jnp.arange(freqs, dtype=jnp.int32)
    shifts = jnp.arange(2 * half_lags, dtype=jnp.int32) - half_lags
    phase = jnp.mod(rows[:, None] * shifts[None, :], period)
    angles = phase.astype(jnp.float32) * (2.0 * math.pi / period)
    return jnp.concatenate([jnp.cos(angles), -jnp.sin(angles)], axis=0)


def lag_halves(freqs, half_lags):
    period = 2 * freqs
    phase = np.mod(np.arange(freqs)[:, None] * (np.arange(2 * half_lags) - half_lags)[None, :], period)
    angles = phase * (2.0 * math.pi / period)
    table = np.concatenate([np.cos(angles), -np.sin(angles)], axis=0)
    high = table.astype(np.float32).astype(ml_dtypes.bfloat16)
    low = (table - high.astype(np.float64)).astype(np.float32).astype(ml_dtypes.bfloat16)
    return np.stack([high, low])


def correlate(source_spec, receiver_spec, lag_table):
    segs = receiver_spec.shape[1]
    freqs = receiver_spec.shape[3]
    real_part = jnp.einsum(
        "pkf,krf->prf", source_spec[0], receiver_spec[0], preferred_element_type=jnp.float32
    ) + jnp.einsum(
        "pkf,krf->prf", source_spec[1], receiver_spec[1], preferred_element_type=jnp.float32
    )
    imag_part = jnp.einsum(
        "pkf,krf->prf", source_spec[0], receiver_spec[1], preferred_element_type=jnp.float32
    ) - jnp.einsum(
        "pkf,krf->prf", source_spec[1], receiver_spec[0], preferred_element_type=jnp.float32
    )
    stacked = jnp.concatenate([real_part, imag_part], axis=-1) * (1.0 / math.sqrt(segs))
    flat = stacked.reshape(-1, 2 * freqs)
    result = jnp.dot(
        flat, lag_table, precision=lax.Precision.HIGHEST, preferred_element_type=jnp.float32
    ) * (1.0 / math.sqrt(freqs))
    return result.reshape(stacked.shape[0], stacked.shape[1], -1)


def shards(spectra, sources):
    whitened = whiten(spectra)
    regrouped = lax.all_to_all(whitened, "seg", split_axis=2, concat_axis=1, tiled=True)
    ch_dev = spectra.shape[2]
    freqs = spectra.shape[3]
    first_row = lax.axis_index("chan") * ch_dev
    lag_table = lag_matrix(freqs, LAGS)
    batches = sources.shape[0]
    results = []
    for batch_no in range(batches):
        local_row = sources[batch_no] - first_row
        onehot = (local_row[:, None] == jnp.arange(ch_dev, dtype=jnp.int32)[None, :]).astype(
            jnp.bfloat16
        )
        local_spec = lax.psum(
            jnp.einsum("pc,xscf->xpsf", onehot, whitened, preferred_element_type=jnp.float32),
            "chan",
        ).astype(jnp.bfloat16)
        source_spec = lax.all_gather(local_spec, "seg", axis=2, tiled=True)
        results.append(correlate(source_spec, regrouped, lag_table))
    return jnp.concatenate(results, axis=0)


CHANS = 8
CHIPS = 4
PLANES = 4


def kernel(spectra, sources, table, out, whs, sel, rs_in, rcv, src, vf, wf, acc, tab,
           rs_s, rs_r, a_s, a_r, z_s, z_r, c_s, c_r, p_s, p_r, t_sem):
    d = lax.axis_index("chan")
    z = lax.axis_index("seg")
    chip, core = d // 2, lax.rem(d, 2)
    segs, rows, freqs = spectra.shape[1:]
    n_src = out.shape[0]
    own = rows // PLANES
    tiles = freqs // 128

    table_in = pltpu.make_async_copy(table, tab, t_sem)
    table_in.start()

    def chan_at(o):
        return lax.rem(d + o, CHANS)

    def seg_at(o):
        return lax.rem(z + o, PLANES)

    def to(src_ref, dst_ref, s, r, where):
        return pltpu.make_async_remote_copy(
            src_ref=src_ref, dst_ref=dst_ref, send_sem=s, recv_sem=r,
            device_id=where, device_id_type=MESH)

    picks = {o: to(sel.at[chan_at(o)], rs_in.at[o], rs_s.at[o], rs_r.at[o], {"chan": chan_at(o)})
             for o in range(1, CHANS)}
    regroup = {o: to(whs.at[seg_at(o)], rcv.at[o], a_s.at[o], a_r.at[o], {"seg": seg_at(o)})
               for o in range(1, PLANES)}
    planes = {o: to(src.at[0, 0, 0], src.at[0, o, 0], z_s.at[o], z_r.at[o], {"seg": seg_at(o)})
              for o in range(1, PLANES)}
    chips = {(y, o): to(src.at[0, y, 0], src.at[0, y, o], c_s.at[y, o], c_r.at[y, o],
                        {"chan": lax.rem(chip + o, CHIPS) * 2 + core})
             for y in range(PLANES) for o in range(1, CHIPS)}
    cores = {(y, o): to(src.at[0, y, o], src.at[1, y, o], p_s.at[y, o], p_r.at[y, o],
                        {"chan": d + 1 - 2 * core})
             for y in range(PLANES) for o in range(CHIPS)}

    barrier = pltpu.get_barrier_semaphore()
    for o in range(1, CHANS):
        pl.semaphore_signal(barrier, inc=1, device_id={"chan": chan_at(o)}, device_id_type=MESH)
    for o in range(1, PLANES):
        pl.semaphore_signal(barrier, inc=1, device_id={"seg": seg_at(o)}, device_id_type=MESH)

    row = lax.broadcasted_iota(jnp.int32, (n_src, rows), 0)
    named = jnp.zeros((n_src, rows), jnp.int32)
    per = sources.shape[1]
    for n in range(n_src):
        named = jnp.where(row == n, sources[n // per, n % per], named)
    held = lax.broadcasted_iota(jnp.int32, (n_src, rows), 1) + d * rows
    onehot = (named == held).astype(jnp.float32).astype(jnp.bfloat16)

    def prepare(k):
        re = spectra[0, k].astype(jnp.float32)
        im = spectra[1, k].astype(jnp.float32)
        inv = lax.rsqrt(jnp.mean(re * re + im * im, axis=-1, keepdims=True) + 1e-06)
        re = (re * inv).astype(jnp.bfloat16)
        im = (im * inv).astype(jnp.bfloat16)
        for c, part in enumerate((re, im)):
            sel[k, c] = jnp.dot(onehot, part, preferred_element_type=jnp.float32).astype(jnp.bfloat16)
        re, im = re.astype(jnp.float32), im.astype(jnp.float32)
        for q in range(PLANES):
            cut = slice(q * own, (q + 1) * own)
            whs[q, k] = jnp.concatenate([re[cut], im[cut]], axis=0).astype(jnp.bfloat16)

    prepare(chan_at(1))
    pl.semaphore_wait(barrier, CHANS - 1 + PLANES - 1)
    picks[1].start()
    for o in range(2, CHANS):
        prepare(chan_at(o))
        picks[o].start()
    prepare(d)
    for o in range(1, PLANES):
        regroup[o].start()

    total = sel[d].astype(jnp.float32)
    for o in range(1, CHANS):
        picks[o].wait_recv()
        total = total + rs_in[o].astype(jnp.float32)
    src[0, 0, 0] = total.astype(jnp.bfloat16)
    for o in range(1, PLANES):
        planes[o].start()
    for o in range(1, CHIPS):
        chips[0, o].start()
    cores[0, 0].start()

    def receivers(y):
        for k in range(segs):
            wf[y, k] = (whs[z, k] if y == 0 else rcv[y, k]).astype(jnp.float32)

    def add(y, s, first):
        side = core if s == 0 else 1 - core
        ks = []
        for o in range(CHIPS):
            vf[o] = src[s, y, o].astype(jnp.float32)
            ks.append(lax.rem(chip - o + CHIPS, CHIPS) * 2 + side)
        for t in range(tiles):
            f = slice(t * 128, (t + 1) * 128)
            g = slice(freqs + t * 128, freqs + (t + 1) * 128)
            c = [wf[y, k, 0:own, f] for k in ks]
            e = [wf[y, k, own:2 * own, f] for k in ks]

            def some(m, carry):
                at = pl.ds(pl.multiple_of(m * 8, 8), 8)
                a8 = [vf[o, 0, at, f] for o in range(CHIPS)]
                b8 = [vf[o, 1, at, f] for o in range(CHIPS)]
                for j in range(8):
                    n = m * 8 + j
                    re = im = None
                    for o in range(CHIPS):
                        a = jnp.broadcast_to(a8[o][j:j + 1], (own, 128))
                        b = jnp.broadcast_to(b8[o][j:j + 1], (own, 128))
                        r, i = a * c[o] + b * e[o], a * e[o] - b * c[o]
                        re, im = (r, i) if o == 0 else (re + r, im + i)
                    if not first:
                        re, im = acc[n, :, f] + re, acc[n, :, g] + im
                    acc[n, :, f] = re
                    acc[n, :, g] = im
                return carry

            lax.fori_loop(0, n_src // 8, some, 0)

    receivers(0)
    for o in range(1, CHIPS):
        chips[0, o].wait_recv()
        cores[0, o].start()
    add(0, 0, True)
    for y in range(1, PLANES):
        planes[y].wait_recv()
        for o in range(1, CHIPS):
            chips[y, o].start()
        cores[y, 0].start()
    for o in range(CHIPS):
        cores[0, o].wait_recv()
    add(0, 1, False)
    for y in range(1, PLANES):
        for o in range(1, CHIPS):
            chips[y, o].wait_recv()
            cores[y, o].start()
        regroup[y].wait_recv()
        receivers(y)
        add(y, 0, False)
        for o in range(CHIPS):
            cores[y, o].wait_recv()
        add(y, 1, False)

    table_in.wait()
    scale = 1.0 / math.sqrt(segs * PLANES) / math.sqrt(freqs)
    step = 8

    def lags(m, carry):
        part = acc[pl.ds(m * step, step)].reshape(step * own, 2 * freqs)
        high = part.astype(jnp.bfloat16)
        low = (part - high.astype(jnp.float32)).astype(jnp.bfloat16)
        dot = functools.partial(jnp.dot, preferred_element_type=jnp.float32)
        result = dot(high, tab[0]) + (dot(low, tab[0]) + dot(high, tab[1]))
        out[pl.ds(m * step, step)] = (result * scale).reshape(step, own, -1)
        return carry

    lax.fori_loop(0, n_src // step, lags, 0)

    for group in (picks, regroup, planes, chips, cores):
        for copy in group.values():
            copy.wait_send()


def fused(spectra, sources):
    _, segs, rows, freqs = spectra.shape
    n_src = sources.shape[0] * sources.shape[1]
    own = rows // PLANES
    bf16, f32 = jnp.bfloat16, jnp.float32
    dma = pltpu.SemaphoreType.DMA
    return pl.pallas_call(
        kernel,
        out_shape=jax.ShapeDtypeStruct((n_src, own, 2 * LAGS), f32),
        in_specs=[
            pl.BlockSpec(memory_space=pltpu.VMEM),
            pl.BlockSpec(memory_space=pltpu.SMEM),
            pl.BlockSpec(memory_space=pl.ANY),
        ],
        out_specs=pl.BlockSpec(memory_space=pltpu.VMEM),
        scratch_shapes=[
            pltpu.VMEM((PLANES, segs, 2 * own, freqs), bf16),
            pltpu.VMEM((segs, 2, n_src, freqs), bf16),
            pltpu.VMEM((CHANS, 2, n_src, freqs), bf16),
            pltpu.VMEM((PLANES, segs, 2 * own, freqs), bf16),
            pltpu.VMEM((2, PLANES, CHIPS, 2, n_src, freqs), bf16),
            pltpu.VMEM((CHIPS, 2, n_src, freqs), f32),
            pltpu.VMEM((PLANES, segs, 2 * own, freqs), f32),
            pltpu.VMEM((n_src, own, 2 * freqs), f32),
            pltpu.VMEM((2, 2 * freqs, 2 * LAGS), bf16),
            dma((CHANS,)), dma((CHANS,)),
            dma((PLANES,)), dma((PLANES,)),
            dma((PLANES,)), dma((PLANES,)),
            dma((PLANES, CHIPS)), dma((PLANES, CHIPS)),
            dma((PLANES, CHIPS)), dma((PLANES, CHIPS)),
            dma,
        ],
        compiler_params=pltpu.CompilerParams(
            collective_id=0, has_side_effects=True, vmem_limit_bytes=40 * 1024 * 1024),
    )(spectra, sources, jnp.asarray(lag_halves(freqs, LAGS)))


def solution(mesh):
    placed = (P(None, "seg", "chan", None), P())
    fits = mesh.shape["chan"] == CHANS and mesh.shape["seg"] == PLANES
    return jax.shard_map(
        fused if fits else shards,
        mesh=mesh,
        in_specs=placed,
        out_specs=P(None, ("chan", "seg"), None),
        check_vma=False,
    )
```

```python
import functools
import math

import jax
import jax.numpy as jnp
import ml_dtypes
import numpy as np
from jax import lax
from jax.experimental import pallas as pl
from jax.experimental.pallas import tpu as pltpu
from jax.sharding import PartitionSpec as P

LAGS = 256
MESH = pl.DeviceIdType.MESH


def whiten(spectra):
    values = spectra.astype(jnp.float32)
    power_mean = jnp.mean(values[0] * values[0] + values[1] * values[1], axis=-1)
    inv_scale = lax.rsqrt(power_mean + 1e-06)
    return (values * inv_scale[None, :, :, None]).astype(jnp.bfloat16)


def lag_matrix(freqs, half_lags):
    period = 2 * freqs
    rows = jnp.arange(freqs, dtype=jnp.int32)
    shifts = jnp.arange(2 * half_lags, dtype=jnp.int32) - half_lags
    phase = jnp.mod(rows[:, None] * shifts[None, :], period)
    angles = phase.astype(jnp.float32) * (2.0 * math.pi / period)
    return jnp.concatenate([jnp.cos(angles), -jnp.sin(angles)], axis=0)


def lag_halves(freqs, half_lags):
    period = 2 * freqs
    phase = np.mod(np.arange(freqs)[:, None] * (np.arange(2 * half_lags) - half_lags)[None, :], period)
    angles = phase * (2.0 * math.pi / period)
    table = np.concatenate([np.cos(angles), -np.sin(angles)], axis=0)
    high = table.astype(np.float32).astype(ml_dtypes.bfloat16)
    low = (table - high.astype(np.float64)).astype(np.float32).astype(ml_dtypes.bfloat16)
    return np.stack([high, low])


def correlate(source_spec, receiver_spec, lag_table):
    segs = receiver_spec.shape[1]
    freqs = receiver_spec.shape[3]
    real_part = jnp.einsum(
        "pkf,krf->prf", source_spec[0], receiver_spec[0], preferred_element_type=jnp.float32
    ) + jnp.einsum(
        "pkf,krf->prf", source_spec[1], receiver_spec[1], preferred_element_type=jnp.float32
    )
    imag_part = jnp.einsum(
        "pkf,krf->prf", source_spec[0], receiver_spec[1], preferred_element_type=jnp.float32
    ) - jnp.einsum(
        "pkf,krf->prf", source_spec[1], receiver_spec[0], preferred_element_type=jnp.float32
    )
    stacked = jnp.concatenate([real_part, imag_part], axis=-1) * (1.0 / math.sqrt(segs))
    flat = stacked.reshape(-1, 2 * freqs)
    result = jnp.dot(
        flat, lag_table, precision=lax.Precision.HIGHEST, preferred_element_type=jnp.float32
    ) * (1.0 / math.sqrt(freqs))
    return result.reshape(stacked.shape[0], stacked.shape[1], -1)


def shards(spectra, sources):
    whitened = whiten(spectra)
    regrouped = lax.all_to_all(whitened, "seg", split_axis=2, concat_axis=1, tiled=True)
    ch_dev = spectra.shape[2]
    freqs = spectra.shape[3]
    first_row = lax.axis_index("chan") * ch_dev
    lag_table = lag_matrix(freqs, LAGS)
    batches = sources.shape[0]
    results = []
    for batch_no in range(batches):
        local_row = sources[batch_no] - first_row
        onehot = (local_row[:, None] == jnp.arange(ch_dev, dtype=jnp.int32)[None, :]).astype(
            jnp.bfloat16
        )
        local_spec = lax.psum(
            jnp.einsum("pc,xscf->xpsf", onehot, whitened, preferred_element_type=jnp.float32),
            "chan",
        ).astype(jnp.bfloat16)
        source_spec = lax.all_gather(local_spec, "seg", axis=2, tiled=True)
        results.append(correlate(source_spec, regrouped, lag_table))
    return jnp.concatenate(results, axis=0)


CHANS = 8
CHIPS = 4
PLANES = 4


def kernel(spectra, sources, table, out, spec, whs, sel, core_in, rs_in, rcv, src, vf, wf, acc, tab,
           i_sem, h_s, h_r, rs_s, rs_r, a_s, a_r, z_s, z_r, c_s, c_r, p_s, p_r, t_sem):
    d = lax.axis_index("chan")
    z = lax.axis_index("seg")
    chip, core = d // 2, lax.rem(d, 2)
    segs, rows, freqs = spec.shape[1:]
    n_src = out.shape[0]
    own = rows // PLANES
    half = segs // 2
    tiles = freqs // 128

    spectra_in = pltpu.make_async_copy(spectra, spec, i_sem)
    spectra_in.start()
    table_in = pltpu.make_async_copy(table, tab, t_sem)
    table_in.start()

    def chip_at(o):
        return lax.rem(chip + o, CHIPS)

    def seg_at(o):
        return lax.rem(z + o, PLANES)

    def to(src_ref, dst_ref, s, r, where):
        return pltpu.make_async_remote_copy(
            src_ref=src_ref, dst_ref=dst_ref, send_sem=s, recv_sem=r,
            device_id=where, device_id_type=MESH)

    partner = {"chan": d + 1 - 2 * core}

    def mate(o):
        return {"chan": chip_at(o) * 2 + core}

    halves = [to(sel.at[1, o], core_in.at[o], h_s.at[o], h_r.at[o], partner) for o in range(CHIPS)]
    picks = {o: to(sel.at[0, o], rs_in.at[o], rs_s.at[o], rs_r.at[o], mate(o)) for o in range(1, CHIPS)}
    regroup = {(o, h): to(whs.at[seg_at(o), pl.ds(h * half, half)], rcv.at[o, pl.ds(h * half, half)],
                          a_s.at[o, h], a_r.at[o, h], {"seg": seg_at(o)})
               for o in range(1, PLANES) for h in range(2)}

    def chips(y, o):
        return to(src.at[0, y, 0], src.at[0, y, o], c_s.at[y, o], c_r.at[y, o], mate(o))

    def cores(y, o):
        return to(src.at[0, y, o], src.at[1, y, o], p_s.at[y, o], p_r.at[y, o], partner)

    def right(y):
        return to(src.at[0, y, 0], src.at[0, y + 1, 0], z_s.at[0, y], z_r.at[y + 1], {"seg": z + 1})

    def left(y):
        there = lax.rem(y + PLANES - 1, PLANES)
        return to(src.at[0, y, 0], src.at[0, there, 0], z_s.at[1, y], z_r.at[there], {"seg": z - 1})

    def relay(y, act):
        from_left = z >= y

        @pl.when(jnp.logical_and(from_left, z < PLANES - 1))
        def _():
            act(right(y))

        from_right = jnp.logical_or(z < y, y == 0)

        @pl.when(jnp.logical_and(from_right, z > 0))
        def _():
            act(left(y))

    first, last = (PLANES - 1 - z) // (PLANES - 1), z // (PLANES - 1)
    y1 = 1 + 2 * first
    y3 = 2 - first + last
    y2 = 6 - y1 - y3

    barrier = pltpu.get_barrier_semaphore()
    pl.semaphore_signal(barrier, inc=1, device_id=partner, device_id_type=MESH)
    for o in range(1, CHIPS):
        pl.semaphore_signal(barrier, inc=1, device_id=mate(o), device_id_type=MESH)
    for o in range(1, PLANES):
        pl.semaphore_signal(barrier, inc=1, device_id={"seg": seg_at(o)}, device_id_type=MESH)

    row = lax.broadcasted_iota(jnp.int32, (n_src, rows), 0)
    named = jnp.zeros((n_src, rows), jnp.int32)
    per = sources.shape[0]
    for n in range(n_src):
        named = jnp.where(row == n, sources[n % per, n // per], named)
    held = lax.broadcasted_iota(jnp.int32, (n_src, rows), 1) + d * rows
    onehot = (named == held).astype(jnp.float32).astype(jnp.bfloat16)

    def prepare(side, o):
        k = chip_at(o) * 2 + (core if side == 0 else 1 - core)
        re = spec[0, k].astype(jnp.float32)
        im = spec[1, k].astype(jnp.float32)
        inv = lax.rsqrt(jnp.mean(re * re + im * im, axis=-1, keepdims=True) + 1e-06)
        re = (re * inv).astype(jnp.bfloat16)
        im = (im * inv).astype(jnp.bfloat16)
        for c, part in enumerate((re, im)):
            picked = jnp.dot(onehot, part, preferred_element_type=jnp.float32)
            sel[side, o, c] = picked.astype(jnp.bfloat16)
        re, im = re.astype(jnp.float32), im.astype(jnp.float32)
        for q in range(PLANES):
            cut = slice(q * own, (q + 1) * own)
            whs[q, k] = jnp.concatenate([re[cut], im[cut]], axis=0).astype(jnp.bfloat16)

    spectra_in.wait()
    order = (1, 2, 3, 0)
    for o in order:
        prepare(1, o)
        if o == 1:
            pl.semaphore_wait(barrier, CHIPS + PLANES - 1)
        halves[o].start()
    for o in order:
        prepare(0, o)
    for o in range(1, PLANES):
        regroup[o, 0].start()

    for o in order:
        halves[o].wait_recv()
        sel[0, o] = (sel[0, o].astype(jnp.float32) + core_in[o].astype(jnp.float32)).astype(jnp.bfloat16)
        if o != 0:
            picks[o].start()
    total = sel[0, 0].astype(jnp.float32)
    for o in range(1, CHIPS):
        picks[o].wait_recv()
        total = total + rs_in[o].astype(jnp.float32)
    src[0, 0, 0] = total.astype(jnp.bfloat16)

    def spread(y):
        relay(y, lambda copy: copy.start())
        for o in range(1, CHIPS):
            chips(y, o).start()
        cores(y, 0).start()

    def spread_far(y):
        pltpu.make_async_remote_copy(
            src_ref=src.at[0, y, 0], dst_ref=src.at[0, y, 0], send_sem=z_s.at[0, y], recv_sem=z_r.at[y],
            device_id={"seg": seg_at(1)}, device_id_type=MESH).wait_recv()
        spread(y)

    def share(y):
        for o in range(1, CHIPS):
            chips(y, o).wait_recv()
            cores(y, o).start()

    def receivers(y):
        for k in range(segs):
            wf[y, k] = (whs[z, k] if type(y) is int else rcv[y, k]).astype(jnp.float32)

    def await_receivers(y):
        for h in range(2):
            at = rcv.at[y, pl.ds(h * half, half)]
            pltpu.make_async_remote_copy(
                src_ref=at, dst_ref=at, send_sem=a_s.at[y, h], recv_sem=a_r.at[y, h],
                device_id={"seg": seg_at(1)}, device_id_type=MESH).wait_recv()
        receivers(y)

    def add(y, s, begin=False):
        if s == 1:
            for o in range(CHIPS):
                cores(y, o).wait_recv()
        side = core if s == 0 else 1 - core
        ks = []
        for o in range(CHIPS):
            vf[o] = src[s, y, o].astype(jnp.float32)
            ks.append(chip_at(CHIPS - o) * 2 + side)
        for t in range(tiles):
            f = slice(t * 128, (t + 1) * 128)
            g = slice(freqs + t * 128, freqs + (t + 1) * 128)
            c = [wf[y, k, 0:own, f] for k in ks]
            e = [wf[y, k, own:2 * own, f] for k in ks]

            def some(m, carry):
                at = pl.ds(pl.multiple_of(m * 8, 8), 8)
                a8 = [vf[o, 0, at, f] for o in range(CHIPS)]
                b8 = [vf[o, 1, at, f] for o in range(CHIPS)]
                for j in range(8):
                    n = m * 8 + j
                    re = im = None
                    for o in range(CHIPS):
                        a = jnp.broadcast_to(a8[o][j:j + 1], (own, 128))
                        b = jnp.broadcast_to(b8[o][j:j + 1], (own, 128))
                        r, i = a * c[o] + b * e[o], a * e[o] - b * c[o]
                        re, im = (r, i) if o == 0 else (re + r, im + i)
                    if not begin:
                        re, im = acc[n, :, f] + re, acc[n, :, g] + im
                    acc[n, :, f] = re
                    acc[n, :, g] = im
                return carry

            lax.fori_loop(0, n_src // 8, some, 0)

    spread(0)
    receivers(0)
    share(0)
    spread_far(y1)
    for o in range(1, PLANES):
        regroup[o, 1].start()
    add(0, 0, True)
    spread_far(y2)
    add(0, 1)
    spread_far(y3)
    share(y1)
    await_receivers(y1)
    add(y1, 0)
    share(y2)
    add(y1, 1)
    await_receivers(y2)
    add(y2, 0)
    share(y3)
    add(y2, 1)
    await_receivers(y3)
    add(y3, 0)
    add(y3, 1)

    table_in.wait()
    scale = 1.0 / math.sqrt(segs * PLANES) / math.sqrt(freqs)
    flat = acc[...].reshape(n_src * own, 2 * freqs)
    high = flat.astype(jnp.bfloat16)
    low = (flat - high.astype(jnp.float32)).astype(jnp.bfloat16)
    dot = functools.partial(jnp.dot, preferred_element_type=jnp.float32)
    result = dot(high, tab[0]) + (dot(low, tab[0]) + dot(high, tab[1]))
    out[...] = (result * scale).reshape(out.shape)

    for copy in (*halves, *picks.values(), *regroup.values()):
        copy.wait_send()
    for y in range(PLANES):
        relay(y, lambda copy: copy.wait_send())
        for o in range(CHIPS):
            if o > 0:
                chips(y, o).wait_send()
            cores(y, o).wait_send()


def fused(spectra, sources):
    _, segs, rows, freqs = spectra.shape
    n_src = sources.shape[0] * sources.shape[1]
    own = rows // PLANES
    bf16, f32 = jnp.bfloat16, jnp.float32
    dma = pltpu.SemaphoreType.DMA
    return pl.pallas_call(
        kernel,
        out_shape=jax.ShapeDtypeStruct((n_src, own, 2 * LAGS), f32),
        in_specs=[
            pl.BlockSpec(memory_space=pl.ANY),
            pl.BlockSpec(memory_space=pltpu.SMEM),
            pl.BlockSpec(memory_space=pl.ANY),
        ],
        out_specs=pl.BlockSpec(memory_space=pltpu.VMEM),
        scratch_shapes=[
            pltpu.VMEM((2, segs, rows, freqs), bf16),
            pltpu.VMEM((PLANES, segs, 2 * own, freqs), bf16),
            pltpu.VMEM((2, CHIPS, 2, n_src, freqs), bf16),
            pltpu.VMEM((CHIPS, 2, n_src, freqs), bf16),
            pltpu.VMEM((CHIPS, 2, n_src, freqs), bf16),
            pltpu.VMEM((PLANES, segs, 2 * own, freqs), bf16),
            pltpu.VMEM((2, PLANES, CHIPS, 2, n_src, freqs), bf16),
            pltpu.VMEM((CHIPS, 2, n_src, freqs), f32),
            pltpu.VMEM((PLANES, segs, 2 * own, freqs), f32),
            pltpu.VMEM((n_src, own, 2 * freqs), f32),
            pltpu.VMEM((2, 2 * freqs, 2 * LAGS), bf16),
            dma,
            dma((CHIPS,)), dma((CHIPS,)),
            dma((CHIPS,)), dma((CHIPS,)),
            dma((PLANES, 2)), dma((PLANES, 2)),
            dma((2, PLANES)), dma((PLANES,)),
            dma((PLANES, CHIPS)), dma((PLANES, CHIPS)),
            dma((PLANES, CHIPS)), dma((PLANES, CHIPS)),
            dma,
        ],
        compiler_params=pltpu.CompilerParams(
            collective_id=0, has_side_effects=True, vmem_limit_bytes=60 * 1024 * 1024),
    )(spectra, sources.T, jnp.asarray(lag_halves(freqs, LAGS)))


def solution(mesh):
    placed = (P(None, "seg", "chan", None), P())
    fits = mesh.shape["chan"] == CHANS and mesh.shape["seg"] == PLANES
    return jax.shard_map(
        fused if fits else shards,
        mesh=mesh,
        in_specs=placed,
        out_specs=P(None, ("chan", "seg"), None),
        check_vma=False,
    )
```

```python
import functools
import math

import jax
import jax.numpy as jnp
import ml_dtypes
import numpy as np
from jax import lax
from jax.experimental import pallas as pl
from jax.experimental.pallas import tpu as pltpu
from jax.sharding import PartitionSpec as P

LAGS = 256
MESH = pl.DeviceIdType.MESH


def whiten(spectra):
    values = spectra.astype(jnp.float32)
    power_mean = jnp.mean(values[0] * values[0] + values[1] * values[1], axis=-1)
    inv_scale = lax.rsqrt(power_mean + 1e-06)
    return (values * inv_scale[None, :, :, None]).astype(jnp.bfloat16)


def lag_matrix(freqs, half_lags):
    period = 2 * freqs
    rows = jnp.arange(freqs, dtype=jnp.int32)
    shifts = jnp.arange(2 * half_lags, dtype=jnp.int32) - half_lags
    phase = jnp.mod(rows[:, None] * shifts[None, :], period)
    angles = phase.astype(jnp.float32) * (2.0 * math.pi / period)
    return jnp.concatenate([jnp.cos(angles), -jnp.sin(angles)], axis=0)


def lag_halves(freqs, half_lags):
    period = 2 * freqs
    phase = np.mod(np.arange(freqs)[:, None] * (np.arange(2 * half_lags) - half_lags)[None, :], period)
    angles = phase * (2.0 * math.pi / period)
    table = np.concatenate([np.cos(angles), -np.sin(angles)], axis=0)
    high = table.astype(np.float32).astype(ml_dtypes.bfloat16)
    low = (table - high.astype(np.float64)).astype(np.float32).astype(ml_dtypes.bfloat16)
    return np.stack([high, low])


def correlate(source_spec, receiver_spec, lag_table):
    segs = receiver_spec.shape[1]
    freqs = receiver_spec.shape[3]
    real_part = jnp.einsum(
        "pkf,krf->prf", source_spec[0], receiver_spec[0], preferred_element_type=jnp.float32
    ) + jnp.einsum(
        "pkf,krf->prf", source_spec[1], receiver_spec[1], preferred_element_type=jnp.float32
    )
    imag_part = jnp.einsum(
        "pkf,krf->prf", source_spec[0], receiver_spec[1], preferred_element_type=jnp.float32
    ) - jnp.einsum(
        "pkf,krf->prf", source_spec[1], receiver_spec[0], preferred_element_type=jnp.float32
    )
    stacked = jnp.concatenate([real_part, imag_part], axis=-1) * (1.0 / math.sqrt(segs))
    flat = stacked.reshape(-1, 2 * freqs)
    result = jnp.dot(
        flat, lag_table, precision=lax.Precision.HIGHEST, preferred_element_type=jnp.float32
    ) * (1.0 / math.sqrt(freqs))
    return result.reshape(stacked.shape[0], stacked.shape[1], -1)


def shards(spectra, sources):
    whitened = whiten(spectra)
    regrouped = lax.all_to_all(whitened, "seg", split_axis=2, concat_axis=1, tiled=True)
    ch_dev = spectra.shape[2]
    freqs = spectra.shape[3]
    first_row = lax.axis_index("chan") * ch_dev
    lag_table = lag_matrix(freqs, LAGS)
    batches = sources.shape[0]
    results = []
    for batch_no in range(batches):
        local_row = sources[batch_no] - first_row
        onehot = (local_row[:, None] == jnp.arange(ch_dev, dtype=jnp.int32)[None, :]).astype(
            jnp.bfloat16
        )
        local_spec = lax.psum(
            jnp.einsum("pc,xscf->xpsf", onehot, whitened, preferred_element_type=jnp.float32),
            "chan",
        ).astype(jnp.bfloat16)
        source_spec = lax.all_gather(local_spec, "seg", axis=2, tiled=True)
        results.append(correlate(source_spec, regrouped, lag_table))
    return jnp.concatenate(results, axis=0)


CHANS = 8
CHIPS = 4
PLANES = 4


def kernel(spectra, sources, table, out, spec, whs, sel, core_in, rs_in, rcv, src, vf, wf, acc, tab,
           i_sem, h_s, h_r, rs_s, rs_r, a_s, a_r, z_s, z_r, c_s, c_r, p_s, p_r, t_sem):
    d = lax.axis_index("chan")
    z = lax.axis_index("seg")
    chip, core = d // 2, lax.rem(d, 2)
    segs, rows, freqs = spec.shape[1:]
    n_src = out.shape[0]
    own = rows // PLANES
    half = segs // 2
    tiles = freqs // 128

    spectra_in = pltpu.make_async_copy(spectra, spec, i_sem)
    spectra_in.start()
    table_in = pltpu.make_async_copy(table, tab, t_sem)
    table_in.start()

    def chip_at(o):
        return lax.rem(chip + o, CHIPS)

    def seg_at(o):
        return lax.rem(z + o, PLANES)

    def to(src_ref, dst_ref, s, r, where):
        return pltpu.make_async_remote_copy(
            src_ref=src_ref, dst_ref=dst_ref, send_sem=s, recv_sem=r,
            device_id=where, device_id_type=MESH)

    partner = {"chan": d + 1 - 2 * core}

    def mate(o):
        return {"chan": chip_at(o) * 2 + core}

    halves = [to(sel.at[1, o], core_in.at[o], h_s.at[o], h_r.at[o], partner) for o in range(CHIPS)]
    picks = {o: to(sel.at[0, o], rs_in.at[o], rs_s.at[o], rs_r.at[o], mate(o)) for o in range(1, CHIPS)}

    def regroup(o, h):
        part = pl.ds(h * half, half)
        return to(whs.at[seg_at(o), part], rcv.at[o, part], a_s.at[o, h], a_r.at[o, h], {"seg": seg_at(o)})

    def chips(y, o):
        return to(src.at[0, y, 0], src.at[0, y, o], c_s.at[y, o], c_r.at[y, o], mate(o))

    def cores(y, o):
        return to(src.at[0, y, o], src.at[1, y, o], p_s.at[y, o], p_r.at[y, o], partner)

    def right(y):
        return to(src.at[0, y, 0], src.at[0, y + 1, 0], z_s.at[0, y], z_r.at[y + 1], {"seg": z + 1})

    def left(y):
        there = lax.rem(y + PLANES - 1, PLANES)
        return to(src.at[0, y, 0], src.at[0, there, 0], z_s.at[1, y], z_r.at[there], {"seg": z - 1})

    def relay(y, act):
        from_left = z >= y

        @pl.when(jnp.logical_and(from_left, z < PLANES - 1))
        def _():
            act(right(y))

        from_right = jnp.logical_or(z < y, y == 0)

        @pl.when(jnp.logical_and(from_right, z > 0))
        def _():
            act(left(y))

    first, last = (PLANES - 1 - z) // (PLANES - 1), z // (PLANES - 1)
    y1 = 1 + 2 * first
    y3 = 2 - first + last
    y2 = 6 - y1 - y3
    far = 2 + first - last
    near = 1 + first + last
    reach = (far, near, 6 - far - near)

    barrier = pltpu.get_barrier_semaphore()
    pl.semaphore_signal(barrier, inc=1, device_id=partner, device_id_type=MESH)
    for o in range(1, CHIPS):
        pl.semaphore_signal(barrier, inc=1, device_id=mate(o), device_id_type=MESH)
    for o in range(1, PLANES):
        pl.semaphore_signal(barrier, inc=1, device_id={"seg": seg_at(o)}, device_id_type=MESH)

    row = lax.broadcasted_iota(jnp.int32, (n_src, rows), 0)
    named = jnp.zeros((n_src, rows), jnp.int32)
    per = sources.shape[0]
    for n in range(n_src):
        named = jnp.where(row == n, sources[n % per, n // per], named)
    held = lax.broadcasted_iota(jnp.int32, (n_src, rows), 1) + d * rows
    onehot = (named == held).astype(jnp.float32).astype(jnp.bfloat16)

    def prepare(side, o):
        k = chip_at(o) * 2 + (core if side == 0 else 1 - core)
        re = spec[0, k].astype(jnp.float32)
        im = spec[1, k].astype(jnp.float32)
        inv = lax.rsqrt(jnp.mean(re * re + im * im, axis=-1, keepdims=True) + 1e-06)
        re = (re * inv).astype(jnp.bfloat16)
        im = (im * inv).astype(jnp.bfloat16)
        for c, part in enumerate((re, im)):
            picked = jnp.dot(onehot, part, preferred_element_type=jnp.float32)
            sel[side, o, c] = picked.astype(jnp.bfloat16)
        re, im = re.astype(jnp.float32), im.astype(jnp.float32)
        for q in range(PLANES):
            cut = slice(q * own, (q + 1) * own)
            whs[q, k] = jnp.concatenate([re[cut], im[cut]], axis=0).astype(jnp.bfloat16)

    spectra_in.wait()
    order = (1, 2, 3, 0)
    for o in order:
        prepare(1, o)
        if o == 1:
            pl.semaphore_wait(barrier, CHIPS + PLANES - 1)
        halves[o].start()
    for o in order:
        prepare(0, o)
    for o in reach:
        regroup(o, 0).start()

    for o in order:
        halves[o].wait_recv()
        sel[0, o] = (sel[0, o].astype(jnp.float32) + core_in[o].astype(jnp.float32)).astype(jnp.bfloat16)
        if o != 0:
            picks[o].start()
    total = sel[0, 0].astype(jnp.float32)
    for o in range(1, CHIPS):
        picks[o].wait_recv()
        total = total + rs_in[o].astype(jnp.float32)
    src[0, 0, 0] = total.astype(jnp.bfloat16)

    def spread(y):
        relay(y, lambda copy: copy.start())
        for o in range(1, CHIPS):
            chips(y, o).start()
        cores(y, 0).start()

    def spread_far(y):
        pltpu.make_async_remote_copy(
            src_ref=src.at[0, y, 0], dst_ref=src.at[0, y, 0], send_sem=z_s.at[0, y], recv_sem=z_r.at[y],
            device_id={"seg": seg_at(1)}, device_id_type=MESH).wait_recv()
        spread(y)

    def share(y):
        for o in range(1, CHIPS):
            chips(y, o).wait_recv()
            cores(y, o).start()

    def receivers(y):
        for k in range(segs):
            wf[y, k] = (whs[z, k] if type(y) is int else rcv[y, k]).astype(jnp.float32)

    def await_receivers(y):
        for h in range(2):
            at = rcv.at[y, pl.ds(h * half, half)]
            pltpu.make_async_remote_copy(
                src_ref=at, dst_ref=at, send_sem=a_s.at[y, h], recv_sem=a_r.at[y, h],
                device_id={"seg": seg_at(1)}, device_id_type=MESH).wait_recv()
        receivers(y)

    def add(y, s, begin=False):
        if s == 1:
            for o in range(CHIPS):
                cores(y, o).wait_recv()
        side = core if s == 0 else 1 - core
        ks = []
        for o in range(CHIPS):
            vf[o] = src[s, y, o].astype(jnp.float32)
            ks.append(chip_at(CHIPS - o) * 2 + side)

        def tile(t, carry):
            f = pl.ds(pl.multiple_of(t * 128, 128), 128)
            g = pl.ds(pl.multiple_of(freqs + t * 128, 128), 128)
            cs = [wf[y, k, 0:own, f] for k in ks]
            es = [wf[y, k, own:2 * own, f] for k in ks]
            for r in range(own):
                c = [jnp.broadcast_to(v[r:r + 1], (8, 128)) for v in cs]
                e = [jnp.broadcast_to(v[r:r + 1], (8, 128)) for v in es]
                for m in range(n_src // 8):
                    n = slice(m * 8, m * 8 + 8)
                    re = im = None
                    for o in range(CHIPS):
                        a, b = vf[o, 0, n, f], vf[o, 1, n, f]
                        u, v = a * c[o] + b * e[o], a * e[o] - b * c[o]
                        re, im = (u, v) if o == 0 else (re + u, im + v)
                    if not begin:
                        re, im = acc[r, n, f] + re, acc[r, n, g] + im
                    acc[r, n, f] = re
                    acc[r, n, g] = im
            return carry

        lax.fori_loop(0, tiles, tile, 0)

    spread(0)
    receivers(0)
    share(0)
    spread_far(y1)
    spread_far(y2)
    for o in reach:
        regroup(o, 1).start()
    add(0, 0, True)
    spread_far(y3)
    add(0, 1)
    share(y1)
    await_receivers(y1)
    add(y1, 0)
    share(y2)
    add(y1, 1)
    await_receivers(y2)
    add(y2, 0)
    share(y3)
    add(y2, 1)
    await_receivers(y3)
    add(y3, 0)
    add(y3, 1)

    table_in.wait()
    scale = 1.0 / math.sqrt(segs * PLANES) / math.sqrt(freqs)
    flat = acc[...].reshape(n_src * own, 2 * freqs)
    high = flat.astype(jnp.bfloat16)
    low = (flat - high.astype(jnp.float32)).astype(jnp.bfloat16)
    dot = functools.partial(jnp.dot, preferred_element_type=jnp.float32)
    result = dot(high, tab[0]) + (dot(low, tab[0]) + dot(high, tab[1]))
    result = result * scale
    for r in range(own):
        out[:, r, :] = result[r * n_src:(r + 1) * n_src]

    for copy in (*halves, *picks.values(), *(regroup(o, h) for o in range(1, PLANES) for h in range(2))):
        copy.wait_send()
    for y in range(PLANES):
        relay(y, lambda copy: copy.wait_send())
        for o in range(CHIPS):
            if o > 0:
                chips(y, o).wait_send()
            cores(y, o).wait_send()


def fused(spectra, sources):
    _, segs, rows, freqs = spectra.shape
    n_src = sources.shape[0] * sources.shape[1]
    own = rows // PLANES
    bf16, f32 = jnp.bfloat16, jnp.float32
    dma = pltpu.SemaphoreType.DMA
    return pl.pallas_call(
        kernel,
        out_shape=jax.ShapeDtypeStruct((n_src, own, 2 * LAGS), f32),
        in_specs=[
            pl.BlockSpec(memory_space=pltpu.HBM),
            pl.BlockSpec(memory_space=pltpu.SMEM),
            pl.BlockSpec(memory_space=pltpu.HBM),
        ],
        out_specs=pl.BlockSpec(memory_space=pltpu.VMEM),
        scratch_shapes=[
            pltpu.VMEM((2, segs, rows, freqs), bf16),
            pltpu.VMEM((PLANES, segs, 2 * own, freqs), bf16),
            pltpu.VMEM((2, CHIPS, 2, n_src, freqs), bf16),
            pltpu.VMEM((CHIPS, 2, n_src, freqs), bf16),
            pltpu.VMEM((CHIPS, 2, n_src, freqs), bf16),
            pltpu.VMEM((PLANES, segs, 2 * own, freqs), bf16),
            pltpu.VMEM((2, PLANES, CHIPS, 2, n_src, freqs), bf16),
            pltpu.VMEM((CHIPS, 2, n_src, freqs), f32),
            pltpu.VMEM((PLANES, segs, 2 * own, freqs), f32),
            pltpu.VMEM((own, n_src, 2 * freqs), f32),
            pltpu.VMEM((2, 2 * freqs, 2 * LAGS), bf16),
            dma,
            dma((CHIPS,)), dma((CHIPS,)),
            dma((CHIPS,)), dma((CHIPS,)),
            dma((PLANES, 2)), dma((PLANES, 2)),
            dma((2, PLANES)), dma((PLANES,)),
            dma((PLANES, CHIPS)), dma((PLANES, CHIPS)),
            dma((PLANES, CHIPS)), dma((PLANES, CHIPS)),
            dma,
        ],
        compiler_params=pltpu.CompilerParams(
            collective_id=0, has_side_effects=True, vmem_limit_bytes=40 * 1024 * 1024),
    )(spectra, sources.T, jnp.asarray(lag_halves(freqs, LAGS)))


def solution(mesh):
    placed = (P(None, "seg", "chan", None), P())
    fits = mesh.shape["chan"] == CHANS and mesh.shape["seg"] == PLANES
    return jax.shard_map(
        fused if fits else shards,
        mesh=mesh,
        in_specs=placed,
        out_specs=P(None, ("chan", "seg"), None),
        check_vma=False,
    )
```

```python
import functools
import math

import jax
import jax.numpy as jnp
import ml_dtypes
import numpy as np
from jax import lax
from jax.experimental import pallas as pl
from jax.experimental.pallas import tpu as pltpu
from jax.sharding import PartitionSpec as P

LAGS = 256
MESH = pl.DeviceIdType.MESH


def whiten(spectra):
    values = spectra.astype(jnp.float32)
    power_mean = jnp.mean(values[0] * values[0] + values[1] * values[1], axis=-1)
    inv_scale = lax.rsqrt(power_mean + 1e-06)
    return (values * inv_scale[None, :, :, None]).astype(jnp.bfloat16)


def lag_matrix(freqs, half_lags):
    period = 2 * freqs
    rows = jnp.arange(freqs, dtype=jnp.int32)
    shifts = jnp.arange(2 * half_lags, dtype=jnp.int32) - half_lags
    phase = jnp.mod(rows[:, None] * shifts[None, :], period)
    angles = phase.astype(jnp.float32) * (2.0 * math.pi / period)
    return jnp.concatenate([jnp.cos(angles), -jnp.sin(angles)], axis=0)


def lag_halves(freqs, half_lags):
    period = 2 * freqs
    phase = np.mod(np.arange(freqs)[:, None] * (np.arange(2 * half_lags) - half_lags)[None, :], period)
    angles = phase * (2.0 * math.pi / period)
    table = np.concatenate([np.cos(angles), -np.sin(angles)], axis=0)
    high = table.astype(np.float32).astype(ml_dtypes.bfloat16)
    low = (table - high.astype(np.float64)).astype(np.float32).astype(ml_dtypes.bfloat16)
    return np.stack([high, low])


def correlate(source_spec, receiver_spec, lag_table):
    segs = receiver_spec.shape[1]
    freqs = receiver_spec.shape[3]
    real_part = jnp.einsum(
        "pkf,krf->prf", source_spec[0], receiver_spec[0], preferred_element_type=jnp.float32
    ) + jnp.einsum(
        "pkf,krf->prf", source_spec[1], receiver_spec[1], preferred_element_type=jnp.float32
    )
    imag_part = jnp.einsum(
        "pkf,krf->prf", source_spec[0], receiver_spec[1], preferred_element_type=jnp.float32
    ) - jnp.einsum(
        "pkf,krf->prf", source_spec[1], receiver_spec[0], preferred_element_type=jnp.float32
    )
    stacked = jnp.concatenate([real_part, imag_part], axis=-1) * (1.0 / math.sqrt(segs))
    flat = stacked.reshape(-1, 2 * freqs)
    result = jnp.dot(
        flat, lag_table, precision=lax.Precision.HIGHEST, preferred_element_type=jnp.float32
    ) * (1.0 / math.sqrt(freqs))
    return result.reshape(stacked.shape[0], stacked.shape[1], -1)


def shards(spectra, sources):
    whitened = whiten(spectra)
    regrouped = lax.all_to_all(whitened, "seg", split_axis=2, concat_axis=1, tiled=True)
    ch_dev = spectra.shape[2]
    freqs = spectra.shape[3]
    first_row = lax.axis_index("chan") * ch_dev
    lag_table = lag_matrix(freqs, LAGS)
    batches = sources.shape[0]
    results = []
    for batch_no in range(batches):
        local_row = sources[batch_no] - first_row
        onehot = (local_row[:, None] == jnp.arange(ch_dev, dtype=jnp.int32)[None, :]).astype(
            jnp.bfloat16
        )
        local_spec = lax.psum(
            jnp.einsum("pc,xscf->xpsf", onehot, whitened, preferred_element_type=jnp.float32),
            "chan",
        ).astype(jnp.bfloat16)
        source_spec = lax.all_gather(local_spec, "seg", axis=2, tiled=True)
        results.append(correlate(source_spec, regrouped, lag_table))
    return jnp.concatenate(results, axis=0)


CHANS = 8
CHIPS = 4
PLANES = 4


def kernel(spectra, sources, table, out, spec, whs, sel, core_in, rs_in, rcv, src, vf, wf, acc, tab,
           i_sem, h_s, h_r, rs_s, rs_r, a_s, a_r, z_s, z_r, c_s, c_r, p_s, p_r, t_sem):
    d = lax.axis_index("chan")
    z = lax.axis_index("seg")
    chip, core = d // 2, lax.rem(d, 2)
    segs, rows, freqs = spec.shape[1:]
    n_src = out.shape[0]
    own = rows // PLANES
    half = segs // 2
    tiles = freqs // 128

    spectra_in = pltpu.make_async_copy(spectra, spec, i_sem)
    spectra_in.start()
    table_in = pltpu.make_async_copy(table, tab, t_sem)
    table_in.start()

    def chip_at(o):
        x_too = 1 - 2 * lax.rem(chip, 2) if o % 2 else 0
        return lax.rem(chip + x_too + (o // 2) * 2, CHIPS)

    def seg_at(o):
        return lax.rem(z + o, PLANES)

    def to(src_ref, dst_ref, s, r, where):
        return pltpu.make_async_remote_copy(
            src_ref=src_ref, dst_ref=dst_ref, send_sem=s, recv_sem=r,
            device_id=where, device_id_type=MESH)

    partner = {"chan": d + 1 - 2 * core}

    def mate(o):
        return {"chan": chip_at(o) * 2 + core}

    halves = [to(sel.at[1, o], core_in.at[o], h_s.at[o], h_r.at[o], partner) for o in range(CHIPS)]
    picks = {o: to(sel.at[0, o], rs_in.at[o], rs_s.at[o], rs_r.at[o], mate(o)) for o in range(1, CHIPS)}

    def regroup(o, h):
        part = pl.ds(h * half, half)
        return to(whs.at[seg_at(o), part], rcv.at[o, part], a_s.at[o, h], a_r.at[o, h], {"seg": seg_at(o)})

    def chips(y, o):
        return to(src.at[0, y, 0], src.at[0, y, o], c_s.at[y, o], c_r.at[y, o], mate(o))

    def across(y, o):
        c = o - 1
        return to(src.at[0, y, o, c], src.at[0, y, 3, c], c_s.at[y, o + 2], c_r.at[y, o + 2], mate(3 - o))

    def cores(y, o):
        return to(src.at[0, y, o], src.at[1, y, o], p_s.at[y, o], p_r.at[y, o], partner)

    def right(y):
        return to(src.at[0, y, 0], src.at[0, y + 1, 0], z_s.at[0, y], z_r.at[y + 1], {"seg": z + 1})

    def left(y):
        there = lax.rem(y + PLANES - 1, PLANES)
        return to(src.at[0, y, 0], src.at[0, there, 0], z_s.at[1, y], z_r.at[there], {"seg": z - 1})

    def relay(y, act):
        from_left = z >= y

        @pl.when(jnp.logical_and(from_left, z < PLANES - 1))
        def _():
            act(right(y))

        from_right = jnp.logical_or(z < y, y == 0)

        @pl.when(jnp.logical_and(from_right, z > 0))
        def _():
            act(left(y))

    first, last = (PLANES - 1 - z) // (PLANES - 1), z // (PLANES - 1)
    y1 = 1 + 2 * first
    y3 = 2 - first + last
    y2 = 6 - y1 - y3
    far = 2 + first - last
    near = 1 + first + last
    reach = (far, near, 6 - far - near)

    barrier = pltpu.get_barrier_semaphore()
    pl.semaphore_signal(barrier, inc=1, device_id=partner, device_id_type=MESH)
    for o in range(1, CHIPS):
        pl.semaphore_signal(barrier, inc=1, device_id=mate(o), device_id_type=MESH)
    for o in range(1, PLANES):
        pl.semaphore_signal(barrier, inc=1, device_id={"seg": seg_at(o)}, device_id_type=MESH)

    row = lax.broadcasted_iota(jnp.int32, (n_src, rows), 0)
    named = jnp.zeros((n_src, rows), jnp.int32)
    per = sources.shape[0]
    for n in range(n_src):
        named = jnp.where(row == n, sources[n % per, n // per], named)
    held = lax.broadcasted_iota(jnp.int32, (n_src, rows), 1) + d * rows
    onehot = (named == held).astype(jnp.float32).astype(jnp.bfloat16)

    def prepare(side, o):
        k = chip_at(o) * 2 + (core if side == 0 else 1 - core)
        re = spec[0, k].astype(jnp.float32)
        im = spec[1, k].astype(jnp.float32)
        inv = lax.rsqrt(jnp.mean(re * re + im * im, axis=-1, keepdims=True) + 1e-06)
        re = (re * inv).astype(jnp.bfloat16)
        im = (im * inv).astype(jnp.bfloat16)
        for c, part in enumerate((re, im)):
            picked = jnp.dot(onehot, part, preferred_element_type=jnp.float32)
            sel[side, o, c] = picked.astype(jnp.bfloat16)
        re, im = re.astype(jnp.float32), im.astype(jnp.float32)
        for q in range(PLANES):
            cut = slice(q * own, (q + 1) * own)
            whs[q, k] = jnp.concatenate([re[cut], im[cut]], axis=0).astype(jnp.bfloat16)

    spectra_in.wait()
    order = (1, 2, 3, 0)
    for o in order:
        prepare(1, o)
        if o == 1:
            pl.semaphore_wait(barrier, CHIPS + PLANES - 1)
        halves[o].start()
    for o in order:
        prepare(0, o)
    for o in reach:
        regroup(o, 0).start()

    for o in order:
        halves[o].wait_recv()
        sel[0, o] = (sel[0, o].astype(jnp.float32) + core_in[o].astype(jnp.float32)).astype(jnp.bfloat16)
        if o != 0:
            picks[o].start()
    total = sel[0, 0].astype(jnp.float32)
    for o in range(1, CHIPS):
        picks[o].wait_recv()
        total = total + rs_in[o].astype(jnp.float32)
    src[0, 0, 0] = total.astype(jnp.bfloat16)

    def spread(y):
        relay(y, lambda copy: copy.start())
        for o in (1, 2):
            chips(y, o).start()
        cores(y, 0).start()

    def spread_far(y):
        pltpu.make_async_remote_copy(
            src_ref=src.at[0, y, 0], dst_ref=src.at[0, y, 0], send_sem=z_s.at[0, y], recv_sem=z_r.at[y],
            device_id={"seg": seg_at(1)}, device_id_type=MESH).wait_recv()
        spread(y)

    def share(y):
        for o in (1, 2):
            chips(y, o).wait_recv()
            across(y, o).start()
            cores(y, o).start()

    def share_across(y):
        for o in (1, 2):
            across(y, o).wait_recv()
        cores(y, 3).start()

    def receivers(y):
        for k in range(segs):
            wf[y, k] = (whs[z, k] if type(y) is int else rcv[y, k]).astype(jnp.float32)

    def await_receivers(y):
        for h in range(2):
            at = rcv.at[y, pl.ds(h * half, half)]
            pltpu.make_async_remote_copy(
                src_ref=at, dst_ref=at, send_sem=a_s.at[y, h], recv_sem=a_r.at[y, h],
                device_id={"seg": seg_at(1)}, device_id_type=MESH).wait_recv()
        receivers(y)

    def add(y, s, begin=False):
        if s == 1:
            for o in range(CHIPS):
                cores(y, o).wait_recv()
        side = core if s == 0 else 1 - core
        ks = []
        for o in range(CHIPS):
            vf[o] = src[s, y, o].astype(jnp.float32)
            ks.append(chip_at(o) * 2 + side)

        def tile(t, carry):
            f = pl.ds(pl.multiple_of(t * 128, 128), 128)
            g = pl.ds(pl.multiple_of(freqs + t * 128, 128), 128)
            cs = [wf[y, k, 0:own, f] for k in ks]
            es = [wf[y, k, own:2 * own, f] for k in ks]
            for r in range(own):
                c = [jnp.broadcast_to(v[r:r + 1], (8, 128)) for v in cs]
                e = [jnp.broadcast_to(v[r:r + 1], (8, 128)) for v in es]
                for m in range(n_src // 8):
                    n = slice(m * 8, m * 8 + 8)
                    re = im = None
                    for o in range(CHIPS):
                        a, b = vf[o, 0, n, f], vf[o, 1, n, f]
                        u, v = a * c[o] + b * e[o], a * e[o] - b * c[o]
                        re, im = (u, v) if o == 0 else (re + u, im + v)
                    if not begin:
                        re, im = acc[r, n, f] + re, acc[r, n, g] + im
                    acc[r, n, f] = re
                    acc[r, n, g] = im
            return carry

        lax.fori_loop(0, tiles, tile, 0)

    spread(0)
    receivers(0)
    share(0)
    spread_far(y1)
    share_across(0)
    spread_far(y2)
    for o in reach:
        regroup(o, 1).start()
    share(y1)
    add(0, 0, True)
    spread_far(y3)
    share(y2)
    share_across(y1)
    add(0, 1)
    share(y3)
    await_receivers(y1)
    add(y1, 0)
    share_across(y2)
    add(y1, 1)
    share_across(y3)
    await_receivers(y2)
    add(y2, 0)
    add(y2, 1)
    await_receivers(y3)
    add(y3, 0)
    add(y3, 1)

    table_in.wait()
    scale = 1.0 / math.sqrt(segs * PLANES) / math.sqrt(freqs)
    flat = acc[...].reshape(n_src * own, 2 * freqs)
    high = flat.astype(jnp.bfloat16)
    low = (flat - high.astype(jnp.float32)).astype(jnp.bfloat16)
    dot = functools.partial(jnp.dot, preferred_element_type=jnp.float32)
    result = dot(high, tab[0]) + (dot(low, tab[0]) + dot(high, tab[1]))
    result = result * scale
    for r in range(own):
        out[:, r, :] = result[r * n_src:(r + 1) * n_src]

    for copy in (*halves, *picks.values(), *(regroup(o, h) for o in range(1, PLANES) for h in range(2))):
        copy.wait_send()
    for y in range(PLANES):
        relay(y, lambda copy: copy.wait_send())
        for o in range(CHIPS):
            if o in (1, 2):
                chips(y, o).wait_send()
                across(y, o).wait_send()
            cores(y, o).wait_send()


def fused(spectra, sources):
    _, segs, rows, freqs = spectra.shape
    n_src = sources.shape[0] * sources.shape[1]
    own = rows // PLANES
    bf16, f32 = jnp.bfloat16, jnp.float32
    dma = pltpu.SemaphoreType.DMA
    return pl.pallas_call(
        kernel,
        out_shape=jax.ShapeDtypeStruct((n_src, own, 2 * LAGS), f32),
        in_specs=[
            pl.BlockSpec(memory_space=pltpu.HBM),
            pl.BlockSpec(memory_space=pltpu.SMEM),
            pl.BlockSpec(memory_space=pltpu.HBM),
        ],
        out_specs=pl.BlockSpec(memory_space=pltpu.VMEM),
        scratch_shapes=[
            pltpu.VMEM((2, segs, rows, freqs), bf16),
            pltpu.VMEM((PLANES, segs, 2 * own, freqs), bf16),
            pltpu.VMEM((2, CHIPS, 2, n_src, freqs), bf16),
            pltpu.VMEM((CHIPS, 2, n_src, freqs), bf16),
            pltpu.VMEM((CHIPS, 2, n_src, freqs), bf16),
            pltpu.VMEM((PLANES, segs, 2 * own, freqs), bf16),
            pltpu.VMEM((2, PLANES, CHIPS, 2, n_src, freqs), bf16),
            pltpu.VMEM((CHIPS, 2, n_src, freqs), f32),
            pltpu.VMEM((PLANES, segs, 2 * own, freqs), f32),
            pltpu.VMEM((own, n_src, 2 * freqs), f32),
            pltpu.VMEM((2, 2 * freqs, 2 * LAGS), bf16),
            dma,
            dma((CHIPS,)), dma((CHIPS,)),
            dma((CHIPS,)), dma((CHIPS,)),
            dma((PLANES, 2)), dma((PLANES, 2)),
            dma((2, PLANES)), dma((PLANES,)),
            dma((PLANES, 5)), dma((PLANES, 5)),
            dma((PLANES, CHIPS)), dma((PLANES, CHIPS)),
            dma,
        ],
        compiler_params=pltpu.CompilerParams(
            collective_id=0, has_side_effects=True, vmem_limit_bytes=60 * 1024 * 1024),
    )(spectra, sources.T, jnp.asarray(lag_halves(freqs, LAGS)))


def solution(mesh):
    placed = (P(None, "seg", "chan", None), P())
    fits = mesh.shape["chan"] == CHANS and mesh.shape["seg"] == PLANES
    return jax.shard_map(
        fused if fits else shards,
        mesh=mesh,
        in_specs=placed,
        out_specs=P(None, ("chan", "seg"), None),
        check_vma=False,
    )
```

```python
import functools
import math

import jax
import jax.numpy as jnp
import ml_dtypes
import numpy as np
from jax import lax
from jax.experimental import pallas as pl
from jax.experimental.pallas import tpu as pltpu
from jax.sharding import PartitionSpec as P

LAGS = 256
MESH = pl.DeviceIdType.MESH


def whiten(spectra):
    values = spectra.astype(jnp.float32)
    power_mean = jnp.mean(values[0] * values[0] + values[1] * values[1], axis=-1)
    inv_scale = lax.rsqrt(power_mean + 1e-06)
    return (values * inv_scale[None, :, :, None]).astype(jnp.bfloat16)


def lag_matrix(freqs, half_lags):
    period = 2 * freqs
    rows = jnp.arange(freqs, dtype=jnp.int32)
    shifts = jnp.arange(2 * half_lags, dtype=jnp.int32) - half_lags
    phase = jnp.mod(rows[:, None] * shifts[None, :], period)
    angles = phase.astype(jnp.float32) * (2.0 * math.pi / period)
    return jnp.concatenate([jnp.cos(angles), -jnp.sin(angles)], axis=0)


def lag_halves(freqs, half_lags):
    period = 2 * freqs
    phase = np.mod(np.arange(freqs)[:, None] * (np.arange(2 * half_lags) - half_lags)[None, :], period)
    angles = phase * (2.0 * math.pi / period)
    table = np.concatenate([np.cos(angles), -np.sin(angles)], axis=0)
    high = table.astype(np.float32).astype(ml_dtypes.bfloat16)
    low = (table - high.astype(np.float64)).astype(np.float32).astype(ml_dtypes.bfloat16)
    return np.stack([high, low])


def correlate(source_spec, receiver_spec, lag_table):
    segs = receiver_spec.shape[1]
    freqs = receiver_spec.shape[3]
    real_part = jnp.einsum(
        "pkf,krf->prf", source_spec[0], receiver_spec[0], preferred_element_type=jnp.float32
    ) + jnp.einsum(
        "pkf,krf->prf", source_spec[1], receiver_spec[1], preferred_element_type=jnp.float32
    )
    imag_part = jnp.einsum(
        "pkf,krf->prf", source_spec[0], receiver_spec[1], preferred_element_type=jnp.float32
    ) - jnp.einsum(
        "pkf,krf->prf", source_spec[1], receiver_spec[0], preferred_element_type=jnp.float32
    )
    stacked = jnp.concatenate([real_part, imag_part], axis=-1) * (1.0 / math.sqrt(segs))
    flat = stacked.reshape(-1, 2 * freqs)
    result = jnp.dot(
        flat, lag_table, precision=lax.Precision.HIGHEST, preferred_element_type=jnp.float32
    ) * (1.0 / math.sqrt(freqs))
    return result.reshape(stacked.shape[0], stacked.shape[1], -1)


def shards(spectra, sources):
    whitened = whiten(spectra)
    regrouped = lax.all_to_all(whitened, "seg", split_axis=2, concat_axis=1, tiled=True)
    ch_dev = spectra.shape[2]
    freqs = spectra.shape[3]
    first_row = lax.axis_index("chan") * ch_dev
    lag_table = lag_matrix(freqs, LAGS)
    batches = sources.shape[0]
    results = []
    for batch_no in range(batches):
        local_row = sources[batch_no] - first_row
        onehot = (local_row[:, None] == jnp.arange(ch_dev, dtype=jnp.int32)[None, :]).astype(
            jnp.bfloat16
        )
        local_spec = lax.psum(
            jnp.einsum("pc,xscf->xpsf", onehot, whitened, preferred_element_type=jnp.float32),
            "chan",
        ).astype(jnp.bfloat16)
        source_spec = lax.all_gather(local_spec, "seg", axis=2, tiled=True)
        results.append(correlate(source_spec, regrouped, lag_table))
    return jnp.concatenate(results, axis=0)


CHANS = 8
CHIPS = 4
PLANES = 4


def kernel(spectra, sources, table, out, spec, whs, sel, core_in, rs_in, rcv, src, vf, wf, acc, tab,
           i_sem, h_s, h_r, rs_s, rs_r, a_s, a_r, z_s, z_r, c_s, c_r, p_s, p_r, t_sem):
    d = lax.axis_index("chan")
    z = lax.axis_index("seg")
    chip, core = d // 2, lax.rem(d, 2)
    segs, rows, freqs = spectra.shape[1:]
    n_src = out.shape[0]
    own = rows // PLANES
    tiles = freqs // 128

    def chip_at(o):
        return lax.rem(chip + o, CHIPS)

    def side_at(side):
        return core if side == 0 else 1 - core

    def segment(side, o):
        k = chip_at(o) * 2 + side_at(side)
        return pltpu.make_async_copy(spectra.at[:, k], spec.at[side, o], i_sem.at[side, o])

    for side in (1, 0):
        for o in range(CHIPS):
            segment(side, o).start()
    table_in = pltpu.make_async_copy(table, tab, t_sem)
    table_in.start()

    def seg_at(o):
        return lax.rem(z + o, PLANES)

    def to(src_ref, dst_ref, s, r, where):
        return pltpu.make_async_remote_copy(
            src_ref=src_ref, dst_ref=dst_ref, send_sem=s, recv_sem=r,
            device_id=where, device_id_type=MESH)

    partner = {"chan": d + 1 - 2 * core}

    def mate(o):
        return {"chan": chip_at(o) * 2 + core}

    halves = to(sel.at[1], core_in, h_s, h_r, partner)
    picks = {o: to(sel.at[0, o], rs_in.at[o], rs_s.at[o], rs_r.at[o], mate(o)) for o in range(1, CHIPS)}

    def regroup(o, h):
        return to(whs.at[seg_at(o), 1 - h], rcv.at[o, 1 - h], a_s.at[o, h], a_r.at[o, h], {"seg": seg_at(o)})

    def chips(y, o):
        return to(src.at[0, y, 0], src.at[0, y, o], c_s.at[y, o], c_r.at[y, o], mate(o))

    def cores(y, o):
        return to(src.at[0, y, o], src.at[1, y, o], p_s.at[y, o], p_r.at[y, o], partner)

    def right(y):
        return to(src.at[0, y, 0], src.at[0, y + 1, 0], z_s.at[0, y], z_r.at[y + 1], {"seg": z + 1})

    def left(y):
        there = lax.rem(y + PLANES - 1, PLANES)
        return to(src.at[0, y, 0], src.at[0, there, 0], z_s.at[1, y], z_r.at[there], {"seg": z - 1})

    def relay(y, act):
        from_left = z >= y

        @pl.when(jnp.logical_and(from_left, z < PLANES - 1))
        def _():
            act(right(y))

        from_right = jnp.logical_or(z < y, y == 0)

        @pl.when(jnp.logical_and(from_right, z > 0))
        def _():
            act(left(y))

    first, last = (PLANES - 1 - z) // (PLANES - 1), z // (PLANES - 1)
    y1 = 1 + 2 * first
    y3 = 2 - first + last
    y2 = 6 - y1 - y3
    far = 2 + first - last
    near = 1 + first + last
    reach = (far, near, 6 - far - near)

    barrier = pltpu.get_barrier_semaphore()
    pl.semaphore_signal(barrier, inc=1, device_id=partner, device_id_type=MESH)
    for o in range(1, CHIPS):
        pl.semaphore_signal(barrier, inc=1, device_id=mate(o), device_id_type=MESH)
    for o in range(1, PLANES):
        pl.semaphore_signal(barrier, inc=1, device_id={"seg": seg_at(o)}, device_id_type=MESH)

    row = lax.broadcasted_iota(jnp.int32, (n_src, rows), 0)
    named = jnp.zeros((n_src, rows), jnp.int32)
    per = sources.shape[0]
    for n in range(n_src):
        named = jnp.where(row == n, sources[n % per, n // per], named)
    held = lax.broadcasted_iota(jnp.int32, (n_src, rows), 1) + d * rows
    onehot = (named == held).astype(jnp.float32).astype(jnp.bfloat16)

    def prepare(side):
        for o in range(CHIPS):
            segment(side, o).wait()
        for o in range(CHIPS):
            re = spec[side, o, 0].astype(jnp.float32)
            im = spec[side, o, 1].astype(jnp.float32)
            inv = lax.rsqrt(jnp.mean(re * re + im * im, axis=-1, keepdims=True) + 1e-06)
            re = (re * inv).astype(jnp.bfloat16)
            im = (im * inv).astype(jnp.bfloat16)
            for c, part in enumerate((re, im)):
                picked = jnp.dot(onehot, part, preferred_element_type=jnp.float32)
                sel[side, o, c] = picked.astype(jnp.bfloat16)
            re, im = re.astype(jnp.float32), im.astype(jnp.float32)
            for q in range(PLANES):
                cut = slice(q * own, (q + 1) * own)
                both = jnp.concatenate([re[cut], im[cut]], axis=0)
                whs[q, side, o] = both.astype(jnp.bfloat16)

    prepare(1)
    pl.semaphore_wait(barrier, CHIPS + PLANES - 1)
    halves.start()
    for o in reach:
        regroup(o, 0).start()
    prepare(0)

    halves.wait_recv()
    for o in (2, 1, 3, 0):
        sel[0, o] = (sel[0, o].astype(jnp.float32) + core_in[o].astype(jnp.float32)).astype(jnp.bfloat16)
        if o != 0:
            picks[o].start()
    total = sel[0, 0].astype(jnp.float32)
    for o in range(1, CHIPS):
        picks[o].wait_recv()
        total = total + rs_in[o].astype(jnp.float32)
    src[0, 0, 0] = total.astype(jnp.bfloat16)

    def spread(y):
        relay(y, lambda copy: copy.start())
        for o in range(1, CHIPS):
            chips(y, o).start()
        cores(y, 0).start()

    def spread_far(y):
        pltpu.make_async_remote_copy(
            src_ref=src.at[0, y, 0], dst_ref=src.at[0, y, 0], send_sem=z_s.at[0, y], recv_sem=z_r.at[y],
            device_id={"seg": seg_at(1)}, device_id_type=MESH).wait_recv()
        spread(y)

    def share(y):
        for o in range(1, CHIPS):
            chips(y, o).wait_recv()
            cores(y, o).start()

    def receivers(y):
        for side in range(2):
            for o in range(CHIPS):
                wf[y, side, o] = (whs[z, side, o] if type(y) is int else rcv[y, side, o]).astype(jnp.float32)

    def await_receivers(y):
        for h in range(2):
            at = rcv.at[y, 1 - h]
            pltpu.make_async_remote_copy(
                src_ref=at, dst_ref=at, send_sem=a_s.at[y, h], recv_sem=a_r.at[y, h],
                device_id={"seg": seg_at(1)}, device_id_type=MESH).wait_recv()
        receivers(y)

    def add(y, s, begin=False):
        if s == 1:
            for o in range(CHIPS):
                cores(y, o).wait_recv()
        ks = []
        for o in range(CHIPS):
            vf[o] = src[s, y, o].astype(jnp.float32)
            ks.append((CHIPS - o) % CHIPS)

        def tile(t, carry):
            f = pl.ds(pl.multiple_of(t * 128, 128), 128)
            g = pl.ds(pl.multiple_of(freqs + t * 128, 128), 128)
            cs = [wf[y, s, k, 0:own, f] for k in ks]
            es = [wf[y, s, k, own:2 * own, f] for k in ks]
            for r in range(own):
                c = [jnp.broadcast_to(v[r:r + 1], (8, 128)) for v in cs]
                e = [jnp.broadcast_to(v[r:r + 1], (8, 128)) for v in es]
                for m in range(n_src // 8):
                    n = slice(m * 8, m * 8 + 8)
                    re = im = None
                    for o in range(CHIPS):
                        a, b = vf[o, 0, n, f], vf[o, 1, n, f]
                        u, v = a * c[o] + b * e[o], a * e[o] - b * c[o]
                        re, im = (u, v) if o == 0 else (re + u, im + v)
                    if not begin:
                        re, im = acc[r, n, f] + re, acc[r, n, g] + im
                    acc[r, n, f] = re
                    acc[r, n, g] = im
            return carry

        lax.fori_loop(0, tiles, tile, 0)

    spread(0)
    receivers(0)
    spread_far(y1)
    share(0)
    spread_far(y2)
    for o in reach:
        regroup(o, 1).start()
    add(0, 0, True)
    spread_far(y3)
    add(0, 1)
    share(y1)
    await_receivers(y1)
    add(y1, 0)
    share(y2)
    add(y1, 1)
    await_receivers(y2)
    add(y2, 0)
    share(y3)
    add(y2, 1)
    await_receivers(y3)
    add(y3, 0)
    add(y3, 1)

    table_in.wait()
    scale = 1.0 / math.sqrt(segs * PLANES) / math.sqrt(freqs)
    flat = acc[...].reshape(n_src * own, 2 * freqs)
    high = flat.astype(jnp.bfloat16)
    low = (flat - high.astype(jnp.float32)).astype(jnp.bfloat16)
    dot = functools.partial(jnp.dot, preferred_element_type=jnp.float32)
    result = dot(high, tab[0]) + (dot(low, tab[0]) + dot(high, tab[1]))
    result = result * scale
    for r in range(own):
        out[:, r, :] = result[r * n_src:(r + 1) * n_src]

    for copy in (halves, *picks.values(), *(regroup(o, h) for o in range(1, PLANES) for h in range(2))):
        copy.wait_send()
    for y in range(PLANES):
        relay(y, lambda copy: copy.wait_send())
        for o in range(CHIPS):
            if o > 0:
                chips(y, o).wait_send()
            cores(y, o).wait_send()


def fused(spectra, sources):
    _, segs, rows, freqs = spectra.shape
    n_src = sources.shape[0] * sources.shape[1]
    own = rows // PLANES
    bf16, f32 = jnp.bfloat16, jnp.float32
    dma = pltpu.SemaphoreType.DMA
    return pl.pallas_call(
        kernel,
        out_shape=jax.ShapeDtypeStruct((n_src, own, 2 * LAGS), f32),
        in_specs=[
            pl.BlockSpec(memory_space=pltpu.HBM),
            pl.BlockSpec(memory_space=pltpu.SMEM),
            pl.BlockSpec(memory_space=pltpu.HBM),
        ],
        out_specs=pl.BlockSpec(memory_space=pltpu.VMEM),
        scratch_shapes=[
            pltpu.VMEM((2, CHIPS, 2, rows, freqs), bf16),
            pltpu.VMEM((PLANES, 2, CHIPS, 2 * own, freqs), bf16),
            pltpu.VMEM((2, CHIPS, 2, n_src, freqs), bf16),
            pltpu.VMEM((CHIPS, 2, n_src, freqs), bf16),
            pltpu.VMEM((CHIPS, 2, n_src, freqs), bf16),
            pltpu.VMEM((PLANES, 2, CHIPS, 2 * own, freqs), bf16),
            pltpu.VMEM((2, PLANES, CHIPS, 2, n_src, freqs), bf16),
            pltpu.VMEM((CHIPS, 2, n_src, freqs), f32),
            pltpu.VMEM((PLANES, 2, CHIPS, 2 * own, freqs), f32),
            pltpu.VMEM((own, n_src, 2 * freqs), f32),
            pltpu.VMEM((2, 2 * freqs, 2 * LAGS), bf16),
            dma((2, CHIPS)),
            dma, dma,
            dma((CHIPS,)), dma((CHIPS,)),
            dma((PLANES, 2)), dma((PLANES, 2)),
            dma((2, PLANES)), dma((PLANES,)),
            dma((PLANES, CHIPS)), dma((PLANES, CHIPS)),
            dma((PLANES, CHIPS)), dma((PLANES, CHIPS)),
            dma,
        ],
        compiler_params=pltpu.CompilerParams(
            collective_id=0, has_side_effects=True, vmem_limit_bytes=60 * 1024 * 1024),
    )(spectra, sources.T, jnp.asarray(lag_halves(freqs, LAGS)))


def solution(mesh):
    placed = (P(None, "seg", "chan", None), P())
    fits = mesh.shape["chan"] == CHANS and mesh.shape["seg"] == PLANES
    return jax.shard_map(
        fused if fits else shards,
        mesh=mesh,
        in_specs=placed,
        out_specs=P(None, ("chan", "seg"), None),
        check_vma=False,
    )
```

```python
import functools
import math

import jax
import jax.numpy as jnp
import ml_dtypes
import numpy as np
from jax import lax
from jax.experimental import pallas as pl
from jax.experimental.pallas import tpu as pltpu
from jax.sharding import PartitionSpec as P

LAGS = 256
MESH = pl.DeviceIdType.MESH


def whiten(spectra):
    values = spectra.astype(jnp.float32)
    power_mean = jnp.mean(values[0] * values[0] + values[1] * values[1], axis=-1)
    inv_scale = lax.rsqrt(power_mean + 1e-06)
    return (values * inv_scale[None, :, :, None]).astype(jnp.bfloat16)


def lag_matrix(freqs, half_lags):
    period = 2 * freqs
    rows = jnp.arange(freqs, dtype=jnp.int32)
    shifts = jnp.arange(2 * half_lags, dtype=jnp.int32) - half_lags
    phase = jnp.mod(rows[:, None] * shifts[None, :], period)
    angles = phase.astype(jnp.float32) * (2.0 * math.pi / period)
    return jnp.concatenate([jnp.cos(angles), -jnp.sin(angles)], axis=0)


def lag_halves(freqs, half_lags):
    period = 2 * freqs
    phase = np.mod(np.arange(freqs)[:, None] * (np.arange(2 * half_lags) - half_lags)[None, :], period)
    angles = phase * (2.0 * math.pi / period)
    table = np.concatenate([np.cos(angles), -np.sin(angles)], axis=0)
    high = table.astype(np.float32).astype(ml_dtypes.bfloat16)
    low = (table - high.astype(np.float64)).astype(np.float32).astype(ml_dtypes.bfloat16)
    return np.stack([high, low])


def correlate(source_spec, receiver_spec, lag_table):
    segs = receiver_spec.shape[1]
    freqs = receiver_spec.shape[3]
    real_part = jnp.einsum(
        "pkf,krf->prf", source_spec[0], receiver_spec[0], preferred_element_type=jnp.float32
    ) + jnp.einsum(
        "pkf,krf->prf", source_spec[1], receiver_spec[1], preferred_element_type=jnp.float32
    )
    imag_part = jnp.einsum(
        "pkf,krf->prf", source_spec[0], receiver_spec[1], preferred_element_type=jnp.float32
    ) - jnp.einsum(
        "pkf,krf->prf", source_spec[1], receiver_spec[0], preferred_element_type=jnp.float32
    )
    stacked = jnp.concatenate([real_part, imag_part], axis=-1) * (1.0 / math.sqrt(segs))
    flat = stacked.reshape(-1, 2 * freqs)
    result = jnp.dot(
        flat, lag_table, precision=lax.Precision.HIGHEST, preferred_element_type=jnp.float32
    ) * (1.0 / math.sqrt(freqs))
    return result.reshape(stacked.shape[0], stacked.shape[1], -1)


def shards(spectra, sources):
    whitened = whiten(spectra)
    regrouped = lax.all_to_all(whitened, "seg", split_axis=2, concat_axis=1, tiled=True)
    ch_dev = spectra.shape[2]
    freqs = spectra.shape[3]
    first_row = lax.axis_index("chan") * ch_dev
    lag_table = lag_matrix(freqs, LAGS)
    batches = sources.shape[0]
    results = []
    for batch_no in range(batches):
        local_row = sources[batch_no] - first_row
        onehot = (local_row[:, None] == jnp.arange(ch_dev, dtype=jnp.int32)[None, :]).astype(
            jnp.bfloat16
        )
        local_spec = lax.psum(
            jnp.einsum("pc,xscf->xpsf", onehot, whitened, preferred_element_type=jnp.float32),
            "chan",
        ).astype(jnp.bfloat16)
        source_spec = lax.all_gather(local_spec, "seg", axis=2, tiled=True)
        results.append(correlate(source_spec, regrouped, lag_table))
    return jnp.concatenate(results, axis=0)


CHANS = 8
CHIPS = 4
PLANES = 4


def kernel(spectra, sources, table, out, spec, whs, sel, core_in, rs_in, rcv, src, vf, wf, acc, tab,
           i_sem, h_s, h_r, rs_s, rs_r, a_s, a_r, z_s, z_r, c_s, c_r, p_s, p_r, t_sem):
    d = lax.axis_index("chan")
    z = lax.axis_index("seg")
    chip, core = d // 2, lax.rem(d, 2)
    segs, rows, freqs = spectra.shape[1:]
    n_src = out.shape[0]
    own = rows // PLANES
    tiles = freqs // 128

    def chip_at(o):
        return lax.rem(chip + o, CHIPS)

    def side_at(side):
        return core if side == 0 else 1 - core

    def segment(side, o):
        k = chip_at(o) * 2 + side_at(side)
        return pltpu.make_async_copy(spectra.at[:, k], spec.at[side, o], i_sem.at[side, o])

    for side in (1, 0):
        for o in range(CHIPS):
            segment(side, o).start()
    table_in = pltpu.make_async_copy(table, tab, t_sem)

    def seg_at(o):
        return lax.rem(z + o, PLANES)

    def to(src_ref, dst_ref, s, r, where):
        return pltpu.make_async_remote_copy(
            src_ref=src_ref, dst_ref=dst_ref, send_sem=s, recv_sem=r,
            device_id=where, device_id_type=MESH)

    partner = {"chan": d + 1 - 2 * core}

    def mate(o):
        return {"chan": chip_at(o) * 2 + core}

    halves = to(sel.at[1], core_in, h_s, h_r, partner)
    picks = {o: to(sel.at[0, o], rs_in.at[o], rs_s.at[o], rs_r.at[o], mate(o)) for o in range(1, CHIPS)}

    def regroup(o, h):
        return to(whs.at[seg_at(o), 1 - h], rcv.at[o, 1 - h], a_s.at[o, h], a_r.at[o, h], {"seg": seg_at(o)})

    def chips(y, o):
        return to(src.at[0, y, 0], src.at[0, y, o], c_s.at[y, o], c_r.at[y, o], mate(o))

    def cores(y, o):
        return to(src.at[0, y, o], src.at[1, y, o], p_s.at[y, o], p_r.at[y, o], partner)

    def right(y):
        return to(src.at[0, y, 0], src.at[0, y + 1, 0], z_s.at[0, y], z_r.at[y + 1], {"seg": z + 1})

    def left(y):
        there = lax.rem(y + PLANES - 1, PLANES)
        return to(src.at[0, y, 0], src.at[0, there, 0], z_s.at[1, y], z_r.at[there], {"seg": z - 1})

    def relay(y, act):
        from_left = z >= y

        @pl.when(jnp.logical_and(from_left, z < PLANES - 1))
        def _():
            act(right(y))

        from_right = jnp.logical_or(z < y, y == 0)

        @pl.when(jnp.logical_and(from_right, z > 0))
        def _():
            act(left(y))

    first, last = (PLANES - 1 - z) // (PLANES - 1), z // (PLANES - 1)
    y1 = 1 + 2 * first
    y3 = 2 - first + last
    y2 = 6 - y1 - y3
    far = 2 + first - last
    near = 1 + first + last
    reach = (far, near, 6 - far - near)

    barrier = pltpu.get_barrier_semaphore()
    pl.semaphore_signal(barrier, inc=1, device_id=partner, device_id_type=MESH)
    for o in range(1, CHIPS):
        pl.semaphore_signal(barrier, inc=1, device_id=mate(o), device_id_type=MESH)
    for o in range(1, PLANES):
        pl.semaphore_signal(barrier, inc=1, device_id={"seg": seg_at(o)}, device_id_type=MESH)

    row = lax.broadcasted_iota(jnp.int32, (n_src, rows), 0)
    named = jnp.zeros((n_src, rows), jnp.int32)
    per = sources.shape[0]
    for n in range(n_src):
        named = jnp.where(row == n, sources[n % per, n // per], named)
    held = lax.broadcasted_iota(jnp.int32, (n_src, rows), 1) + d * rows
    onehot = (named == held).astype(jnp.float32).astype(jnp.bfloat16)

    def prepare(side):
        for o in range(CHIPS):
            segment(side, o).wait()
        for o in range(CHIPS):
            re = spec[side, o, 0].astype(jnp.float32)
            im = spec[side, o, 1].astype(jnp.float32)
            inv = lax.rsqrt(jnp.mean(re * re + im * im, axis=-1, keepdims=True) + 1e-06)
            re = (re * inv).astype(jnp.bfloat16)
            im = (im * inv).astype(jnp.bfloat16)
            for c, part in enumerate((re, im)):
                picked = jnp.dot(onehot, part, preferred_element_type=jnp.float32)
                sel[side, o, c] = picked.astype(jnp.bfloat16)
            re, im = re.astype(jnp.float32), im.astype(jnp.float32)
            for q in range(PLANES):
                cut = slice(q * own, (q + 1) * own)
                both = jnp.concatenate([re[cut], im[cut]], axis=0)
                whs[q, side, o] = both.astype(jnp.bfloat16)

    prepare(1)
    pl.semaphore_wait(barrier, CHIPS + PLANES - 1)
    halves.start()
    table_in.start()
    for o in reach:
        regroup(o, 0).start()
    prepare(0)

    halves.wait_recv()
    for o in (2, 1, 3, 0):
        sel[0, o] = (sel[0, o].astype(jnp.float32) + core_in[o].astype(jnp.float32)).astype(jnp.bfloat16)
        if o != 0:
            picks[o].start()
    total = sel[0, 0].astype(jnp.float32)
    for o in range(1, CHIPS):
        picks[o].wait_recv()
        total = total + rs_in[o].astype(jnp.float32)
    src[0, 0, 0] = total.astype(jnp.bfloat16)

    def spread(y):
        relay(y, lambda copy: copy.start())
        for o in range(1, CHIPS):
            chips(y, o).start()
        cores(y, 0).start()

    def spread_far(y):
        pltpu.make_async_remote_copy(
            src_ref=src.at[0, y, 0], dst_ref=src.at[0, y, 0], send_sem=z_s.at[0, y], recv_sem=z_r.at[y],
            device_id={"seg": seg_at(1)}, device_id_type=MESH).wait_recv()
        spread(y)

    def share(y):
        for o in range(1, CHIPS):
            chips(y, o).wait_recv()
            cores(y, o).start()

    def receivers(y):
        for side in range(2):
            for o in range(CHIPS):
                wf[y, side, o] = (whs[z, side, o] if type(y) is int else rcv[y, side, o]).astype(jnp.float32)

    def await_receivers(y):
        for h in range(2):
            at = rcv.at[y, 1 - h]
            pltpu.make_async_remote_copy(
                src_ref=at, dst_ref=at, send_sem=a_s.at[y, h], recv_sem=a_r.at[y, h],
                device_id={"seg": seg_at(1)}, device_id_type=MESH).wait_recv()
        receivers(y)

    def add(y, s, begin=False):
        if s == 1:
            for o in range(CHIPS):
                cores(y, o).wait_recv()
        ks = []
        for o in range(CHIPS):
            vf[o] = src[s, y, o].astype(jnp.float32)
            ks.append((CHIPS - o) % CHIPS)

        def tile(t, carry):
            f = pl.ds(pl.multiple_of(t * 128, 128), 128)
            g = pl.ds(pl.multiple_of(freqs + t * 128, 128), 128)
            cs = [wf[y, s, k, 0:own, f] for k in ks]
            es = [wf[y, s, k, own:2 * own, f] for k in ks]
            for r in range(own):
                c = [jnp.broadcast_to(v[r:r + 1], (8, 128)) for v in cs]
                e = [jnp.broadcast_to(v[r:r + 1], (8, 128)) for v in es]
                for m in range(n_src // 8):
                    n = slice(m * 8, m * 8 + 8)
                    re = im = None
                    for o in range(CHIPS):
                        a, b = vf[o, 0, n, f], vf[o, 1, n, f]
                        u, v = a * c[o] + b * e[o], a * e[o] - b * c[o]
                        re, im = (u, v) if o == 0 else (re + u, im + v)
                    if not begin:
                        re, im = acc[r, n, f] + re, acc[r, n, g] + im
                    acc[r, n, f] = re
                    acc[r, n, g] = im
            return carry

        lax.fori_loop(0, tiles, tile, 0)

    spread(0)
    spread_far(y1)
    spread_far(y2)
    share(0)
    for o in reach:
        regroup(o, 1).start()
    receivers(0)

    at_end = first + last

    @pl.when(at_end == 1)
    def _():
        add(0, 0, True)

    spread_far(y3)

    @pl.when(at_end == 0)
    def _():
        add(0, 0, True)

    share(y1)
    add(0, 1)
    share(y2)
    await_receivers(y1)
    add(y1, 0)
    add(y1, 1)
    share(y3)
    await_receivers(y2)
    add(y2, 0)
    add(y2, 1)
    await_receivers(y3)
    add(y3, 0)
    add(y3, 1)

    table_in.wait()
    scale = 1.0 / math.sqrt(segs * PLANES) / math.sqrt(freqs)
    flat = acc[...].reshape(n_src * own, 2 * freqs)
    high = flat.astype(jnp.bfloat16)
    low = (flat - high.astype(jnp.float32)).astype(jnp.bfloat16)
    dot = functools.partial(jnp.dot, preferred_element_type=jnp.float32)
    result = dot(high, tab[0]) + (dot(low, tab[0]) + dot(high, tab[1]))
    result = result * scale
    for r in range(own):
        out[:, r, :] = result[r * n_src:(r + 1) * n_src]

    for copy in (halves, *picks.values(), *(regroup(o, h) for o in range(1, PLANES) for h in range(2))):
        copy.wait_send()
    for y in range(PLANES):
        relay(y, lambda copy: copy.wait_send())
        for o in range(CHIPS):
            if o > 0:
                chips(y, o).wait_send()
            cores(y, o).wait_send()


def fused(spectra, sources):
    _, segs, rows, freqs = spectra.shape
    n_src = sources.shape[0] * sources.shape[1]
    own = rows // PLANES
    bf16, f32 = jnp.bfloat16, jnp.float32
    dma = pltpu.SemaphoreType.DMA
    return pl.pallas_call(
        kernel,
        out_shape=jax.ShapeDtypeStruct((n_src, own, 2 * LAGS), f32),
        in_specs=[
            pl.BlockSpec(memory_space=pltpu.HBM),
            pl.BlockSpec(memory_space=pltpu.SMEM),
            pl.BlockSpec(memory_space=pltpu.HBM),
        ],
        out_specs=pl.BlockSpec(memory_space=pltpu.VMEM),
        scratch_shapes=[
            pltpu.VMEM((2, CHIPS, 2, rows, freqs), bf16),
            pltpu.VMEM((PLANES, 2, CHIPS, 2 * own, freqs), bf16),
            pltpu.VMEM((2, CHIPS, 2, n_src, freqs), bf16),
            pltpu.VMEM((CHIPS, 2, n_src, freqs), bf16),
            pltpu.VMEM((CHIPS, 2, n_src, freqs), bf16),
            pltpu.VMEM((PLANES, 2, CHIPS, 2 * own, freqs), bf16),
            pltpu.VMEM((2, PLANES, CHIPS, 2, n_src, freqs), bf16),
            pltpu.VMEM((CHIPS, 2, n_src, freqs), f32),
            pltpu.VMEM((PLANES, 2, CHIPS, 2 * own, freqs), f32),
            pltpu.VMEM((own, n_src, 2 * freqs), f32),
            pltpu.VMEM((2, 2 * freqs, 2 * LAGS), bf16),
            dma((2, CHIPS)),
            dma, dma,
            dma((CHIPS,)), dma((CHIPS,)),
            dma((PLANES, 2)), dma((PLANES, 2)),
            dma((2, PLANES)), dma((PLANES,)),
            dma((PLANES, CHIPS)), dma((PLANES, CHIPS)),
            dma((PLANES, CHIPS)), dma((PLANES, CHIPS)),
            dma,
        ],
        compiler_params=pltpu.CompilerParams(
            collective_id=0, has_side_effects=True, vmem_limit_bytes=60 * 1024 * 1024),
    )(spectra, sources.T, jnp.asarray(lag_halves(freqs, LAGS)))


def solution(mesh):
    placed = (P(None, "seg", "chan", None), P())
    fits = mesh.shape["chan"] == CHANS and mesh.shape["seg"] == PLANES
    return jax.shard_map(
        fused if fits else shards,
        mesh=mesh,
        in_specs=placed,
        out_specs=P(None, ("chan", "seg"), None),
        check_vma=False,
    )
```

```python
import functools
import math

import jax
import jax.numpy as jnp
import ml_dtypes
import numpy as np
from jax import lax
from jax.experimental import pallas as pl
from jax.experimental.pallas import tpu as pltpu
from jax.sharding import PartitionSpec as P

LAGS = 256
MESH = pl.DeviceIdType.MESH


def whiten(spectra):
    values = spectra.astype(jnp.float32)
    power_mean = jnp.mean(values[0] * values[0] + values[1] * values[1], axis=-1)
    inv_scale = lax.rsqrt(power_mean + 1e-06)
    return (values * inv_scale[None, :, :, None]).astype(jnp.bfloat16)


def lag_matrix(freqs, half_lags):
    period = 2 * freqs
    rows = jnp.arange(freqs, dtype=jnp.int32)
    shifts = jnp.arange(2 * half_lags, dtype=jnp.int32) - half_lags
    phase = jnp.mod(rows[:, None] * shifts[None, :], period)
    angles = phase.astype(jnp.float32) * (2.0 * math.pi / period)
    return jnp.concatenate([jnp.cos(angles), -jnp.sin(angles)], axis=0)


def lag_halves(freqs, half_lags):
    period = 2 * freqs
    phase = np.mod(np.arange(freqs)[:, None] * (np.arange(2 * half_lags) - half_lags)[None, :], period)
    angles = phase * (2.0 * math.pi / period)
    table = np.concatenate([np.cos(angles), -np.sin(angles)], axis=0)
    high = table.astype(np.float32).astype(ml_dtypes.bfloat16)
    low = (table - high.astype(np.float64)).astype(np.float32).astype(ml_dtypes.bfloat16)
    return np.stack([high, low])


def correlate(source_spec, receiver_spec, lag_table):
    segs = receiver_spec.shape[1]
    freqs = receiver_spec.shape[3]
    real_part = jnp.einsum(
        "pkf,krf->prf", source_spec[0], receiver_spec[0], preferred_element_type=jnp.float32
    ) + jnp.einsum(
        "pkf,krf->prf", source_spec[1], receiver_spec[1], preferred_element_type=jnp.float32
    )
    imag_part = jnp.einsum(
        "pkf,krf->prf", source_spec[0], receiver_spec[1], preferred_element_type=jnp.float32
    ) - jnp.einsum(
        "pkf,krf->prf", source_spec[1], receiver_spec[0], preferred_element_type=jnp.float32
    )
    stacked = jnp.concatenate([real_part, imag_part], axis=-1) * (1.0 / math.sqrt(segs))
    flat = stacked.reshape(-1, 2 * freqs)
    result = jnp.dot(
        flat, lag_table, precision=lax.Precision.HIGHEST, preferred_element_type=jnp.float32
    ) * (1.0 / math.sqrt(freqs))
    return result.reshape(stacked.shape[0], stacked.shape[1], -1)


def shards(spectra, sources):
    whitened = whiten(spectra)
    regrouped = lax.all_to_all(whitened, "seg", split_axis=2, concat_axis=1, tiled=True)
    ch_dev = spectra.shape[2]
    freqs = spectra.shape[3]
    first_row = lax.axis_index("chan") * ch_dev
    lag_table = lag_matrix(freqs, LAGS)
    batches = sources.shape[0]
    results = []
    for batch_no in range(batches):
        local_row = sources[batch_no] - first_row
        onehot = (local_row[:, None] == jnp.arange(ch_dev, dtype=jnp.int32)[None, :]).astype(
            jnp.bfloat16
        )
        local_spec = lax.psum(
            jnp.einsum("pc,xscf->xpsf", onehot, whitened, preferred_element_type=jnp.float32),
            "chan",
        ).astype(jnp.bfloat16)
        source_spec = lax.all_gather(local_spec, "seg", axis=2, tiled=True)
        results.append(correlate(source_spec, regrouped, lag_table))
    return jnp.concatenate(results, axis=0)


CHANS = 8
CHIPS = 4
PLANES = 4


def kernel(spectra, sources, table, out, spec, whs, sel, core_in, rs_in, rcv, src, vf, wf, acc, tab,
           i_sem, h_s, h_r, rs_s, rs_r, a_s, a_r, z_s, z_r, c_s, c_r, p_s, p_r, t_sem):
    d = lax.axis_index("chan")
    z = lax.axis_index("seg")
    chip, core = d // 2, lax.rem(d, 2)
    segs, rows, freqs = spectra.shape[1:]
    n_src = out.shape[0]
    own = rows // PLANES
    tiles = freqs // 128

    def chip_at(o):
        return lax.rem(chip + o, CHIPS)

    def side_at(side):
        return core if side == 0 else 1 - core

    def segment(side, o):
        k = chip_at(o) * 2 + side_at(side)
        return pltpu.make_async_copy(spectra.at[:, k], spec.at[side, o], i_sem.at[side, o])

    for side in (1, 0):
        for o in range(CHIPS):
            segment(side, o).start()
    table_in = pltpu.make_async_copy(table, tab, t_sem)

    def seg_at(o):
        return lax.rem(z + o, PLANES)

    def to(src_ref, dst_ref, s, r, where):
        return pltpu.make_async_remote_copy(
            src_ref=src_ref, dst_ref=dst_ref, send_sem=s, recv_sem=r,
            device_id=where, device_id_type=MESH)

    partner = {"chan": d + 1 - 2 * core}

    def mate(o):
        return {"chan": chip_at(o) * 2 + core}

    halves = to(sel.at[1], core_in, h_s, h_r, partner)
    picks = {o: to(sel.at[0, o], rs_in.at[o], rs_s.at[o], rs_r.at[o], mate(o)) for o in range(1, CHIPS)}

    def regroup(o, h):
        return to(whs.at[seg_at(o), 1 - h], rcv.at[o, 1 - h], a_s.at[o, h], a_r.at[o, h], {"seg": seg_at(o)})

    def chips(y, o):
        return to(src.at[0, y, 0], src.at[0, y, o], c_s.at[y, o], c_r.at[y, o], mate(o))

    def cores(y, o):
        return to(src.at[0, y, o], src.at[1, y, o], p_s.at[y, o], p_r.at[y, o], partner)

    def right(y):
        return to(src.at[0, y, 0], src.at[0, y + 1, 0], z_s.at[0, y], z_r.at[y + 1], {"seg": z + 1})

    def left(y):
        there = lax.rem(y + PLANES - 1, PLANES)
        return to(src.at[0, y, 0], src.at[0, there, 0], z_s.at[1, y], z_r.at[there], {"seg": z - 1})

    def relay(y, act):
        from_left = z >= y

        @pl.when(jnp.logical_and(from_left, z < PLANES - 1))
        def _():
            act(right(y))

        from_right = jnp.logical_or(z < y, y == 0)

        @pl.when(jnp.logical_and(from_right, z > 0))
        def _():
            act(left(y))

    first, last = (PLANES - 1 - z) // (PLANES - 1), z // (PLANES - 1)
    y1 = 1 + 2 * first
    y3 = 2 - first + last
    y2 = 6 - y1 - y3
    far = 2 + first - last
    near = 1 + first + last
    reach = (far, near, 6 - far - near)

    barrier = pltpu.get_barrier_semaphore()
    pl.semaphore_signal(barrier, inc=1, device_id=partner, device_id_type=MESH)
    for o in range(1, CHIPS):
        pl.semaphore_signal(barrier, inc=1, device_id=mate(o), device_id_type=MESH)
    for o in range(1, PLANES):
        pl.semaphore_signal(barrier, inc=1, device_id={"seg": seg_at(o)}, device_id_type=MESH)

    row = lax.broadcasted_iota(jnp.int32, (n_src, rows), 0)
    named = jnp.zeros((n_src, rows), jnp.int32)
    per = sources.shape[0]
    for n in range(n_src):
        named = jnp.where(row == n, sources[n % per, n // per], named)
    held = lax.broadcasted_iota(jnp.int32, (n_src, rows), 1) + d * rows
    onehot = (named == held).astype(jnp.float32).astype(jnp.bfloat16)

    def prepare(side):
        for o in range(CHIPS):
            segment(side, o).wait()
        for o in range(CHIPS):
            re = spec[side, o, 0].astype(jnp.float32)
            im = spec[side, o, 1].astype(jnp.float32)
            inv = lax.rsqrt(jnp.mean(re * re + im * im, axis=-1, keepdims=True) + 1e-06)
            re = (re * inv).astype(jnp.bfloat16)
            im = (im * inv).astype(jnp.bfloat16)
            for c, part in enumerate((re, im)):
                picked = jnp.dot(onehot, part, preferred_element_type=jnp.float32)
                sel[side, o, c] = picked.astype(jnp.bfloat16)
            re, im = re.astype(jnp.float32), im.astype(jnp.float32)
            for q in range(PLANES):
                cut = slice(q * own, (q + 1) * own)
                both = jnp.concatenate([re[cut], im[cut]], axis=0)
                whs[q, side, o] = both.astype(jnp.bfloat16)

    prepare(1)
    pl.semaphore_wait(barrier, CHIPS + PLANES - 1)
    halves.start()
    table_in.start()
    for o in reach:
        regroup(o, 0).start()
    prepare(0)

    halves.wait_recv()
    for o in (2, 1, 3, 0):
        sel[0, o] = (sel[0, o].astype(jnp.float32) + core_in[o].astype(jnp.float32)).astype(jnp.bfloat16)
        if o != 0:
            picks[o].start()
    total = sel[0, 0].astype(jnp.float32)
    for o in range(1, CHIPS):
        picks[o].wait_recv()
        total = total + rs_in[o].astype(jnp.float32)
    src[0, 0, 0] = total.astype(jnp.bfloat16)

    def spread(y):
        relay(y, lambda copy: copy.start())
        for o in range(1, CHIPS):
            chips(y, o).start()
        cores(y, 0).start()

    def spread_far(y):
        pltpu.make_async_remote_copy(
            src_ref=src.at[0, y, 0], dst_ref=src.at[0, y, 0], send_sem=z_s.at[0, y], recv_sem=z_r.at[y],
            device_id={"seg": seg_at(1)}, device_id_type=MESH).wait_recv()
        spread(y)

    def share(y):
        for o in range(1, CHIPS):
            chips(y, o).wait_recv()
            cores(y, o).start()

    def receivers(y):
        for side in range(2):
            for o in range(CHIPS):
                wf[y, side, o] = (whs[z, side, o] if type(y) is int else rcv[y, side, o]).astype(jnp.float32)

    def await_receivers(y):
        for h in range(2):
            at = rcv.at[y, 1 - h]
            pltpu.make_async_remote_copy(
                src_ref=at, dst_ref=at, send_sem=a_s.at[y, h], recv_sem=a_r.at[y, h],
                device_id={"seg": seg_at(1)}, device_id_type=MESH).wait_recv()
        receivers(y)

    def add(y, s, begin=False):
        if s == 1:
            for o in range(CHIPS):
                cores(y, o).wait_recv()
        ks = []
        for o in range(CHIPS):
            vf[o] = src[s, y, o].astype(jnp.float32)
            ks.append((CHIPS - o) % CHIPS)

        def tile(t, carry):
            f = pl.ds(pl.multiple_of(t * 128, 128), 128)
            g = pl.ds(pl.multiple_of(freqs + t * 128, 128), 128)
            cs = [wf[y, s, k, 0:own, f] for k in ks]
            es = [wf[y, s, k, own:2 * own, f] for k in ks]
            for r in range(own):
                c = [jnp.broadcast_to(v[r:r + 1], (8, 128)) for v in cs]
                e = [jnp.broadcast_to(v[r:r + 1], (8, 128)) for v in es]
                for m in range(n_src // 8):
                    n = slice(m * 8, m * 8 + 8)
                    re = im = None
                    for o in range(CHIPS):
                        a, b = vf[o, 0, n, f], vf[o, 1, n, f]
                        u, v = a * c[o] + b * e[o], a * e[o] - b * c[o]
                        re, im = (u, v) if o == 0 else (re + u, im + v)
                    if not begin:
                        re, im = acc[r, n, f] + re, acc[r, n, g] + im
                    acc[r, n, f] = re
                    acc[r, n, g] = im
            return carry

        lax.fori_loop(0, tiles, tile, 0)

    spread(0)
    spread_far(y1)
    spread_far(y2)
    share(0)
    receivers(0)

    at_end = first + last

    @pl.when(at_end == 1)
    def _():
        for o in reach:
            regroup(o, 1).start()
        add(0, 0, True)

    spread_far(y3)

    @pl.when(at_end == 0)
    def _():
        for o in reach:
            regroup(o, 1).start()
        add(0, 0, True)

    share(y1)
    add(0, 1)
    share(y2)
    await_receivers(y1)
    add(y1, 0)
    add(y1, 1)
    share(y3)
    await_receivers(y2)
    add(y2, 0)
    add(y2, 1)
    await_receivers(y3)
    add(y3, 0)
    add(y3, 1)

    table_in.wait()
    scale = 1.0 / math.sqrt(segs * PLANES) / math.sqrt(freqs)
    flat = acc[...].reshape(n_src * own, 2 * freqs)
    high = flat.astype(jnp.bfloat16)
    low = (flat - high.astype(jnp.float32)).astype(jnp.bfloat16)
    dot = functools.partial(jnp.dot, preferred_element_type=jnp.float32)
    result = dot(high, tab[0]) + (dot(low, tab[0]) + dot(high, tab[1]))
    result = result * scale
    for r in range(own):
        out[:, r, :] = result[r * n_src:(r + 1) * n_src]

    for copy in (halves, *picks.values(), *(regroup(o, h) for o in range(1, PLANES) for h in range(2))):
        copy.wait_send()
    for y in range(PLANES):
        relay(y, lambda copy: copy.wait_send())
        for o in range(CHIPS):
            if o > 0:
                chips(y, o).wait_send()
            cores(y, o).wait_send()


def fused(spectra, sources):
    _, segs, rows, freqs = spectra.shape
    n_src = sources.shape[0] * sources.shape[1]
    own = rows // PLANES
    bf16, f32 = jnp.bfloat16, jnp.float32
    dma = pltpu.SemaphoreType.DMA
    return pl.pallas_call(
        kernel,
        out_shape=jax.ShapeDtypeStruct((n_src, own, 2 * LAGS), f32),
        in_specs=[
            pl.BlockSpec(memory_space=pltpu.HBM),
            pl.BlockSpec(memory_space=pltpu.SMEM),
            pl.BlockSpec(memory_space=pltpu.HBM),
        ],
        out_specs=pl.BlockSpec(memory_space=pltpu.VMEM),
        scratch_shapes=[
            pltpu.VMEM((2, CHIPS, 2, rows, freqs), bf16),
            pltpu.VMEM((PLANES, 2, CHIPS, 2 * own, freqs), bf16),
            pltpu.VMEM((2, CHIPS, 2, n_src, freqs), bf16),
            pltpu.VMEM((CHIPS, 2, n_src, freqs), bf16),
            pltpu.VMEM((CHIPS, 2, n_src, freqs), bf16),
            pltpu.VMEM((PLANES, 2, CHIPS, 2 * own, freqs), bf16),
            pltpu.VMEM((2, PLANES, CHIPS, 2, n_src, freqs), bf16),
            pltpu.VMEM((CHIPS, 2, n_src, freqs), f32),
            pltpu.VMEM((PLANES, 2, CHIPS, 2 * own, freqs), f32),
            pltpu.VMEM((own, n_src, 2 * freqs), f32),
            pltpu.VMEM((2, 2 * freqs, 2 * LAGS), bf16),
            dma((2, CHIPS)),
            dma, dma,
            dma((CHIPS,)), dma((CHIPS,)),
            dma((PLANES, 2)), dma((PLANES, 2)),
            dma((2, PLANES)), dma((PLANES,)),
            dma((PLANES, CHIPS)), dma((PLANES, CHIPS)),
            dma((PLANES, CHIPS)), dma((PLANES, CHIPS)),
            dma,
        ],
        compiler_params=pltpu.CompilerParams(
            collective_id=0, has_side_effects=True, vmem_limit_bytes=60 * 1024 * 1024),
    )(spectra, sources.T, jnp.asarray(lag_halves(freqs, LAGS)))


def solution(mesh):
    placed = (P(None, "seg", "chan", None), P())
    fits = mesh.shape["chan"] == CHANS and mesh.shape["seg"] == PLANES
    return jax.shard_map(
        fused if fits else shards,
        mesh=mesh,
        in_specs=placed,
        out_specs=P(None, ("chan", "seg"), None),
        check_vma=False,
    )
```
